128 devices in a mesh: rows: 16 (over z, y), cols: 8 (over x, core).
Axes of the slice: x: 4, y: 4, z: 4, core: 2. Of those that a mesh axis runs over, the one named last changes fastest.
Arguments:
- noise: bfloat16 [6144, 4096], P('rows'), may hold values from -19 to 19
- data: bfloat16 [6144, 4096], P('cols'), may hold values from -6 to 6
- times: float32 [6144], P('rows'), may hold values from 0 to 1
- time_embed: float32 [4096], replicated, may hold values from -4 to 4
- norm_gain: float32 [4096], replicated, may hold values from 0.1 to 1.9
- w_in: bfloat16 [4096, 8192], P('rows', 'cols'), may hold values from -0.09375 to 0.09375
- w_out: bfloat16 [8192, 4096], P('cols', 'rows'), may hold values from -0.0625 to 0.0625
Outputs:
- target: bfloat16 [6144, 4096], P('rows', 'cols')
- grad_in: bfloat16 [4096, 8192], P('rows', 'cols')
- grad_out: bfloat16 [8192, 4096], P('cols', 'rows')
The draws below stay inside these ranges and needn't reach their ends.
All inputs are finite; a program needn't handle non-finite values.
Results may differ from the reference program's by a relative error of at most 0.018.
Values may be sent and summed in bfloat16 or wider, within the bound.
A program may use at most 128 MiB of HBM per device.

```python
import math
import jax
import jax.numpy as jnp
from jax import lax

D = 4096
FF = 8192
ROWS_DEV = 384
ITERS = 3
TOKENS = 6144
DATA_DEV = 768
N_ROWS = 16
N_COLS = 8


def draw_noise(key, part):
    key = jax.random.fold_in(key, 11)
    first = jax.random.fold_in(key, 0)
    values = jnp.clip(jax.random.normal(first, (TOKENS, D), jnp.float32), -6.0, 6.0)
    return values.astype(jnp.bfloat16)


def steps_of(rng, dims, cuts, low, top_value):
    factor_of = 1.0
    for axis_at, parts in cuts:
        steps = jax.random.uniform(jax.random.fold_in(jax.random.fold_in(rng, 6), axis_at), (parts,), jnp.float32, low / len(cuts), top_value / len(cuts))
        factor_of = factor_of * jnp.repeat(jnp.exp(steps), dims[axis_at] // parts).reshape((-1,) + (1,) * (len(dims) - 1 - axis_at))
    return factor_of


def normal_values(stream_key, shape, deviation, reach, shards=(), kind=jnp.bfloat16):
    drawn = jax.random.normal(stream_key, shape, jnp.float32) * deviation
    if len(shards) > 0:
        drawn = steps_of(stream_key, shape, shards, -0.22, 0.18) * drawn
    return jnp.clip(drawn, min=-reach, max=reach).astype(kind)


def setup_inputs(seed: int = 0) -> dict:
    splits = jax.random.split(jax.random.key(seed), 8)
    return {
        "noise": draw_noise(jax.random.fold_in(splits[7], 71), 0),
        "data": normal_values(splits[1], (TOKENS, D), 1.0, 6.0, ((0, 8),)),
        "times": jnp.clip(1.0 * jax.random.uniform(splits[2], (TOKENS,), jnp.float32) ** steps_of(splits[2], (TOKENS,), ((0, 16),), -0.2, 0.2), 0.0, 1.0),
        "time_embed": normal_values(splits[3], (D,), 1.0, 4.0, (), jnp.float32),
        "norm_gain": jnp.clip(1.0 + 0.18 * jax.random.normal(splits[4], (D,), jnp.float32), 0.1, 1.9),
        "w_in": normal_values(splits[5], (D, FF), D ** -0.5, 0.09375, ((0, 16), (1, 8))),
        "w_out": normal_values(splits[6], (FF, D), FF ** -0.5, 0.0625, ((0, 8), (1, 16))),
    }


EPSILON = 0.01

def merge_log(logits, axis):
    top = lax.optimization_barrier(jnp.max(logits, axis=axis, keepdims=True))
    return jnp.squeeze(top, axis) + jnp.log(lax.optimization_barrier(jnp.sum(jnp.exp(logits - top), axis=axis)))

def reference(noise, data, times, time_embed, norm_gain, w_in, w_out):
    noise_f = noise.astype(jnp.float32)
    data_f = data.astype(jnp.float32)
    noise_sq = lax.optimization_barrier(jnp.sum(noise_f * noise_f, axis=1))
    data_sq = lax.optimization_barrier(jnp.sum(data_f * data_f, axis=1))
    cross = lax.dot_general(noise, data, (((1,), (1,)), ((), ())), preferred_element_type=jnp.float32)
    cost = (noise_sq[:, None] + data_sq[None, :] - 2.0 * cross) / D
    base = -EPSILON * math.log(TOKENS)
    row_pot = jnp.zeros((TOKENS,), jnp.float32)
    col_pot = jnp.zeros((TOKENS,), jnp.float32)
    for sweep in range(ITERS):
        col_pot = base - EPSILON * merge_log((row_pot[:, None] - cost) / EPSILON, 0)
        row_pot = base - EPSILON * merge_log((col_pot[None, :] - cost) / EPSILON, 1)
    coupling = (float(TOKENS) * jnp.exp((row_pot[:, None] + col_pot[None, :] - cost) / EPSILON)).astype(jnp.bfloat16)

    def add_target(total, block):
        start = (block * DATA_DEV).astype(jnp.int32)
        piece = lax.dynamic_slice_in_dim(coupling, start, DATA_DEV, 1)
        rows_block = lax.dynamic_slice_in_dim(data, start, DATA_DEV, 0)
        term = jnp.dot(piece, rows_block, preferred_element_type=jnp.float32).astype(jnp.bfloat16)
        term = lax.optimization_barrier(term)
        return (total + term.astype(jnp.float32), None)
    target_f, _ = lax.scan(add_target, jnp.zeros((TOKENS, D), jnp.float32), jnp.arange(N_COLS, dtype=jnp.int32))
    target = target_f.astype(jnp.bfloat16)
    target_v = target.astype(jnp.float32)
    flow = target_v - noise_f
    state = (1.0 - times[:, None]) * noise_f + times[:, None] * target_v + times[:, None] * time_embed[None, :]
    normed = (state * lax.rsqrt(lax.optimization_barrier(jnp.mean(state * state, axis=1, keepdims=True)) + 1e-06) * norm_gain[None, :]).astype(jnp.bfloat16)
    hidden = jnp.dot(normed, w_in, preferred_element_type=jnp.float32)
    active = jax.nn.gelu(hidden, approximate=True).astype(jnp.bfloat16)
    ff_block = FF // N_COLS

    def add_velocity(total, block):
        start = (block * ff_block).astype(jnp.int32)
        piece = lax.dynamic_slice_in_dim(active, start, ff_block, 1)
        weight_block = lax.dynamic_slice_in_dim(w_out, start, ff_block, 0)
        term = jnp.dot(piece, weight_block, preferred_element_type=jnp.float32).astype(jnp.bfloat16)
        term = lax.optimization_barrier(term)
        return (total + term.astype(jnp.float32), None)
    mixed, _ = lax.scan(add_velocity, jnp.zeros((TOKENS, D), jnp.float32), jnp.arange(N_COLS, dtype=jnp.int32))
    velocity = state + mixed
    slope = ((velocity - flow) / math.sqrt(TOKENS)).astype(jnp.bfloat16)
    back = lax.dot_general(slope, w_out, (((1,), (1,)), ((), ())), preferred_element_type=jnp.float32)
    _, pullback = jax.vjp(lambda value: jax.nn.gelu(value, approximate=True), hidden)
    slope_hidden = pullback(back)[0].astype(jnp.bfloat16)

    def block_grad(left, right, shape):

        def add_grad(total, block):
            start = (block * ROWS_DEV).astype(jnp.int32)
            left_block = lax.dynamic_slice_in_dim(left, start, ROWS_DEV, 0)
            right_block = lax.dynamic_slice_in_dim(right, start, ROWS_DEV, 0)
            term = lax.dot_general(left_block, right_block, (((0,), (0,)), ((), ())), preferred_element_type=jnp.float32).astype(jnp.bfloat16)
            term = lax.optimization_barrier(term)
            return (total + term.astype(jnp.float32), None)
        summed, _ = lax.scan(add_grad, jnp.zeros(shape, jnp.float32), jnp.arange(N_ROWS, dtype=jnp.int32))
        return summed.astype(jnp.bfloat16)
    grad_out = block_grad(active, slope, (FF, D))
    grad_in = block_grad(normed, slope_hidden, (D, FF))
    return (target, grad_in, grad_out)
```

```python
import functools
import math

import jax
import jax.numpy as jnp
from jax import lax
from jax.experimental import pallas as pl
from jax.experimental.pallas import tpu as pltpu
from jax.sharding import PartitionSpec as P

ITERS = 3
EPSILON = 0.01
MESH = pl.DeviceIdType.MESH


def sinkhorn_kernel(tokens, n_rows, n_cols, noise_ref, data_ref, p_ref, a_ref, csend, crecv, rsend, rrecv,
                    cs_sem, cr_sem, rs_sem, rr_sem):
    row = lax.axis_index("rows")
    col = lax.axis_index("cols")
    n, width = noise_ref.shape
    m = data_ref.shape[0]

    barrier = pltpu.get_barrier_semaphore()
    for d in range(1, n_rows):
        pl.semaphore_signal(barrier, inc=1, device_id=(lax.rem(row + d, n_rows), col), device_id_type=MESH)
    for d in range(1, n_cols):
        pl.semaphore_signal(barrier, inc=1, device_id=(row, lax.rem(col + d, n_cols)), device_id_type=MESH)

    step = 512
    a_ref[...] = jnp.zeros_like(a_ref)

    def body(k, carry):
        nsq, dsq = carry
        at = pl.ds(pl.multiple_of(k * step, step), step)
        nk = noise_ref[:, at]
        dk = data_ref[:, at]
        a_ref[...] += lax.dot_general(nk, dk, (((1,), (1,)), ((), ())), preferred_element_type=jnp.float32)
        nf = nk.astype(jnp.float32)
        df = dk.astype(jnp.float32)
        nf = nf * nf
        df = df * df
        for j in range(step // 128):
            nsq = nsq + nf[:, j * 128 : (j + 1) * 128]
            dsq = dsq + df[:, j * 128 : (j + 1) * 128]
        return nsq, dsq

    nsq, dsq = lax.fori_loop(
        0, width // step, body, (jnp.zeros((n, 128), jnp.float32), jnp.zeros((m, 128), jnp.float32))
    )
    noise_sq = jnp.sum(nsq, axis=1, keepdims=True)
    data_sq = jnp.sum(dsq.T, axis=0, keepdims=True)
    a_ref[...] = (noise_sq + data_sq - 2.0 * a_ref[...]) * (1.0 / (width * EPSILON))
    base = -math.log(tokens)

    pl.semaphore_wait(barrier, n_rows + n_cols - 2)

    f = jnp.zeros((n, 1), jnp.float32)
    copies = []
    for it in range(ITERS):
        x = f - a_ref[...]
        top = jnp.max(x, axis=0, keepdims=True)
        tot = jnp.sum(jnp.exp(x - top), axis=0, keepdims=True)
        csend[it, 0:1, :] = top
        csend[it, 1:2, :] = tot
        now = []
        for d in range(1, n_rows):
            c = pltpu.make_async_remote_copy(
                src_ref=csend.at[it], dst_ref=crecv.at[it, d - 1],
                send_sem=cs_sem.at[it, d - 1], recv_sem=cr_sem.at[it, d - 1],
                device_id=(lax.rem(row + d, n_rows), col), device_id_type=MESH)
            c.start()
            now.append(c)
        for c in now:
            c.wait_recv()
        copies += now
        got = crecv[it]
        gt = got[:, 0, :]
        best = jnp.maximum(top, jnp.max(gt, axis=0, keepdims=True))
        total = tot * jnp.exp(top - best) + jnp.sum(got[:, 1, :] * jnp.exp(gt - best), axis=0, keepdims=True)
        g = base - (best + jnp.log(total))

        x = g - a_ref[...]
        top = jnp.max(x, axis=1, keepdims=True)
        tot = jnp.sum(jnp.exp(x - top), axis=1, keepdims=True)
        lane = lax.broadcasted_iota(jnp.int32, (n, 128), 1)
        both = jnp.where(lane < 64, top, tot).T
        top = both[0:1]
        tot = both[64:65]
        rsend[it, 0:1, :] = top
        rsend[it, 1:2, :] = tot
        now = []
        for d in range(1, n_cols):
            c = pltpu.make_async_remote_copy(
                src_ref=rsend.at[it], dst_ref=rrecv.at[it, d - 1],
                send_sem=rs_sem.at[it, d - 1], recv_sem=rr_sem.at[it, d - 1],
                device_id=(row, lax.rem(col + d, n_cols)), device_id_type=MESH)
            c.start()
            now.append(c)
        for c in now:
            c.wait_recv()
        copies += now
        got = rrecv[it]
        gt = got[:, 0, :]
        best = jnp.maximum(top, jnp.max(gt, axis=0, keepdims=True))
        total = tot * jnp.exp(top - best) + jnp.sum(got[:, 1, :] * jnp.exp(gt - best), axis=0, keepdims=True)
        f = jnp.broadcast_to(base - (best + jnp.log(total)), (128, n)).T[:, 0:1]
    p_ref[...] = (float(tokens) * jnp.exp(f + g - a_ref[...])).astype(jnp.bfloat16)
    for c in copies:
        c.wait_send()


def couple(noise, data, n_rows, n_cols):
    n, width = noise.shape
    m = data.shape[0]
    vm = pl.BlockSpec(memory_space=pltpu.VMEM)
    return pl.pallas_call(
        functools.partial(sinkhorn_kernel, n * n_rows, n_rows, n_cols),
        out_shape=jax.ShapeDtypeStruct((n, m), jnp.bfloat16),
        in_specs=[vm] * 2,
        out_specs=vm,
        scratch_shapes=[
            pltpu.VMEM((n, m), jnp.float32),
            pltpu.VMEM((ITERS, 2, m), jnp.float32),
            pltpu.VMEM((ITERS, n_rows - 1, 2, m), jnp.float32),
            pltpu.VMEM((ITERS, 2, n), jnp.float32),
            pltpu.VMEM((ITERS, n_cols - 1, 2, n), jnp.float32),
            pltpu.SemaphoreType.DMA((ITERS, n_rows - 1)),
            pltpu.SemaphoreType.DMA((ITERS, n_rows - 1)),
            pltpu.SemaphoreType.DMA((ITERS, n_cols - 1)),
            pltpu.SemaphoreType.DMA((ITERS, n_cols - 1)),
        ],
        compiler_params=pltpu.CompilerParams(
            collective_id=0, has_side_effects=True, vmem_limit_bytes=40 * 2**20
        ),
        cost_estimate=pl.CostEstimate(flops=2 * n * m * width * 30, bytes_accessed=2 * (n + m) * width, transcendentals=7 * n * m),
    )(noise, data)


def per_device(noise, data, times, time_embed, norm_gain, w_in, w_out):
    width = noise.shape[1]
    n_rows = lax.axis_size("rows")
    tokens = noise.shape[0] * n_rows
    col_count = lax.axis_size("cols")
    col_index = lax.axis_index("cols")
    noise_f = noise.astype(jnp.float32)
    coupling = couple(noise, data, n_rows, col_count)
    partial_target = jnp.dot(coupling, data, preferred_element_type=jnp.float32)
    share_width = width // col_count
    target = lax.psum(partial_target.astype(jnp.bfloat16), "cols")
    target_out = lax.dynamic_slice_in_dim(target, col_index * share_width, share_width, 1)
    target_v = target.astype(jnp.float32)
    flow = target_v - noise_f
    state = (
        (1.0 - times[:, None]) * noise_f
        + times[:, None] * target_v
        + times[:, None] * time_embed[None, :]
    )
    normed = (
        state
        * lax.rsqrt(jnp.mean(state * state, axis=1, keepdims=True) + 1e-06)
        * norm_gain[None, :]
    ).astype(jnp.bfloat16)
    hidden = jnp.dot(
        normed, lax.all_gather(w_in, "rows", axis=0, tiled=True), preferred_element_type=jnp.float32
    )
    active = jax.nn.gelu(hidden, approximate=True).astype(jnp.bfloat16)
    w_out_whole = lax.all_gather(w_out, "rows", axis=1, tiled=True)
    partial_velocity = jnp.dot(active, w_out_whole, preferred_element_type=jnp.float32)
    root = math.sqrt(tokens)
    velocity = state + lax.psum(partial_velocity.astype(jnp.bfloat16), "cols").astype(jnp.float32)
    slope = ((velocity - flow) / root).astype(jnp.bfloat16)
    back = lax.dot_general(
        slope, w_out_whole, (((1,), (1,)), ((), ())), preferred_element_type=jnp.float32
    )
    _, pullback = jax.vjp(lambda value: jax.nn.gelu(value, approximate=True), hidden)
    slope_hidden = pullback(back)[0].astype(jnp.bfloat16)
    out_terms = lax.dot_general(
        active, slope, (((0,), (0,)), ((), ())), preferred_element_type=jnp.float32
    )
    grad_out = lax.psum_scatter(
        out_terms.astype(jnp.bfloat16), "rows", scatter_dimension=1, tiled=True
    )
    grad_in = lax.psum_scatter(
        lax.dot_general(
            normed, slope_hidden, (((0,), (0,)), ((), ())), preferred_element_type=jnp.float32
        ).astype(jnp.bfloat16),
        "rows",
        scatter_dimension=0,
        tiled=True,
    )
    return (target_out, grad_in, grad_out)


def solution(mesh):
    in_specs = (
        P("rows", None),
        P("cols", None),
        P("rows"),
        P(),
        P(),
        P("rows", "cols"),
        P("cols", "rows"),
    )
    out_specs = (P("rows", "cols"), P("rows", "cols"), P("cols", "rows"))
    return jax.shard_map(
        per_device, mesh=mesh, in_specs=in_specs, out_specs=out_specs, check_vma=False
    )
```

```python
import functools
import math

import jax
import jax.numpy as jnp
from jax import lax
from jax.experimental import pallas as pl
from jax.experimental.pallas import tpu as pltpu
from jax.sharding import PartitionSpec as P

ITERS = 3
EPSILON = 0.01
MESH = pl.DeviceIdType.MESH
F32 = jnp.float32
BF16 = jnp.bfloat16
NT = (((1,), (1,)), ((), ()))
ORDER = (2, 1, 3, 0)


def ring(value):
    return lax.rem(value + 4, 4)


def tall(row, rows):
    return jnp.broadcast_to(row, (128, rows)).T[:, 0:1]


def flat(left, right):
    lane = lax.broadcasted_iota(jnp.int32, (left.shape[0], 128), 1)
    both = jnp.where(lane < 64, left, right).T
    return both[0:1], both[64:65]


def kernel(noise_hbm, data_hbm, times_ref, embed_ref, gain_ref, w_in_hbm, w_out_ref,
           target_ref, gin_ref, gout_ref,
           slopes, dbuf, win, wout, rx, latents, act, hid, back, a_ref, p_ref, state, sh, turned,
           sibs, sibr, xo, xp, xm, rh, rf, own,
           csend, crecv, rsend, rrecv,
           cs, cr, rs, rr, ag_s, ag_r, xs, xr, ug_s, ug_r, gr_s, gr_r, loc, credit):
    n_rows, n_cols = 16, 8
    row = lax.axis_index("rows")
    col = lax.axis_index("cols")
    z, y = row // 4, lax.rem(row, 4)
    xx, core = col // 2, lax.rem(col, 2)
    n, width = noise_hbm.shape
    m = data_hbm.shape[0]
    share = width // n_cols
    wr, ffd = w_in_hbm.shape
    hw = wr // 2
    qw = wr // 4
    hn = n // 2
    tokens = n * n_rows

    def rcopy(src, dst, send, recv, to):
        c = pltpu.make_async_remote_copy(src_ref=src, dst_ref=dst, send_sem=send, recv_sem=recv,
                                         device_id=to, device_id_type=MESH)
        c.start()
        return c

    barrier = pltpu.get_barrier_semaphore()
    for d in range(1, n_rows):
        pl.semaphore_signal(barrier, inc=1, device_id=(lax.rem(row + d, n_rows), col), device_id_type=MESH)
    for d in range(1, n_cols):
        pl.semaphore_signal(barrier, inc=1, device_id=(row, lax.rem(col + d, n_cols)), device_id_type=MESH)

    def mine(i):
        return pl.ds(pl.multiple_of(i * wr, wr), wr)

    w_copy = pltpu.make_async_copy(w_in_hbm, win.at[mine(row)], loc.at[0])
    w_copy.start()

    def noise_copy(q):
        return pltpu.make_async_copy(noise_hbm.at[:, pl.ds(pl.multiple_of(q * share, share), share)],
                                     slopes.at[q], loc.at[1 + q])

    def data_copy(q):
        return pltpu.make_async_copy(data_hbm.at[:, pl.ds(pl.multiple_of(q * 2 * share, 2 * share), 2 * share)],
                                     dbuf.at[pl.ds(pl.multiple_of(q * m, m), m)], loc.at[9 + q])

    for q in range(4):
        noise_copy(2 * q).start()
        noise_copy(2 * q + 1).start()
        data_copy(q).start()
    wout[mine(row)] = w_out_ref[...].astype(F32).T.astype(BF16)
    w_copy.wait()

    def place(path, f, s):
        return s * 4 + f if path == 0 else f * 4 + s

    def here(path):
        return (y, z) if path == 0 else (z, y)

    def piece(ref, path, f, s, part=None):
        off = path * hw + (qw if part == 1 else 0)
        size = hw if part is None else qw
        return ref.at[pl.ds(pl.multiple_of(place(path, ring(f), ring(s)) * wr + off, qw), size)]

    def toward(path, axis, d):
        f, s = here(path)
        if axis == "f":
            return (place(path, ring(f + d), s), col)
        return (place(path, f, ring(s + d)), col)

    gathers = {}

    def gather_round(w, step):
        ref = (win, wout)[w]
        jobs = {
            1: [(0, "f", 1, 0, 0, None), (1, "f", -1, 0, 0, None), (2, "s", 1, 0, 0, None), (3, "s", -1, 0, 0, None)],
            2: [(4, "f", 1, -1, 0, 0), (5, "f", -1, 1, 0, 1),
                (6, "s", 1, -1, 0, None), (7, "s", -1, -1, 0, None), (8, "s", 1, 1, 0, None), (9, "s", -1, 1, 0, None),
                (10, "s", 1, 0, -1, 0), (11, "s", -1, 0, 1, 1)],
            3: [(12, "s", 1, 2, 0, None), (13, "s", -1, 2, 0, None),
                (14, "s", 1, -1, -1, 0), (15, "s", -1, -1, 1, 1), (16, "s", 1, 1, -1, 0), (17, "s", -1, 1, 1, 1)],
            4: [(18, "s", 1, 2, -1, 0), (19, "s", -1, 2, 1, 1)],
        }
        earlier = {1: (), 2: range(0, 4), 3: range(4, 12), 4: range(12, 18), 5: range(18, 20)}[step]
        for path in range(2):
            for i in earlier:
                gathers[w, path, i].wait_recv()
        for job in jobs.get(step, ()):
            for path in range(2):
                i, axis, d, df, ds_, part = job
                f, s = here(path)
                at = piece(ref, path, f + df, s + ds_, part)
                gathers[w, path, i] = rcopy(at, at, ag_s.at[w, path, i], ag_r.at[w, path, i], toward(path, axis, d))

    pl.semaphore_wait(barrier, n_rows + n_cols - 2)
    gather_round(0, 1)

    a_ref[...] = jnp.zeros_like(a_ref)

    def cost_step(q, carry):
        nsq, dsq = carry
        noise_copy(2 * q).wait()
        noise_copy(2 * q + 1).wait()
        data_copy(q).wait()
        for h in range(2):
            nk = slopes[2 * q + h]
            dk = dbuf[pl.ds(pl.multiple_of(q * m, m), m), h * share : (h + 1) * share]
            a_ref[...] += lax.dot_general(nk, dk, NT, preferred_element_type=F32)
            nf = nk.astype(F32)
            df = dk.astype(F32)
            nf = nf * nf
            df = df * df
            for j in range(share // 128):
                nsq = nsq + nf[:, j * 128 : (j + 1) * 128]
                dsq = dsq + df[:, j * 128 : (j + 1) * 128]
        return nsq, dsq

    nsq, dsq = lax.fori_loop(0, 4, cost_step, (jnp.zeros((n, 128), F32), jnp.zeros((m, 128), F32)))
    noise_sq = jnp.sum(nsq, axis=1, keepdims=True)
    data_sq = jnp.sum(dsq.T, axis=0, keepdims=True)
    a_ref[...] = (noise_sq + data_sq - 2.0 * a_ref[...]) * (1.0 / (width * EPSILON))
    base = -math.log(tokens)
    gather_round(0, 2)
    gather_round(1, 1)

    def rows_swap(it):
        for d in range(1, n_rows):
            rcopy(csend.at[it], crecv.at[it, d - 1], cs.at[it], cr.at[it], (lax.rem(row + d, n_rows), col))

    def cols_swap(it):
        for d in range(1, n_cols):
            rcopy(rsend.at[it], rrecv.at[it, d - 1], rs.at[it], rr.at[it], (row, lax.rem(col + d, n_cols)))

    def await_all(ref, sem):
        pltpu.make_async_copy(ref, ref, sem).wait()

    def merge(got, top, tot):
        gt = got[:, 0, :]
        best = jnp.maximum(top, jnp.max(gt, axis=0, keepdims=True))
        total = tot * jnp.exp(top - best) + jnp.sum(got[:, 1, :] * jnp.exp(gt - best), axis=0, keepdims=True)
        return base - (best + jnp.log(total))

    f = jnp.zeros((n, 1), F32)
    g = None
    for it in range(ITERS):
        x = f - a_ref[...]
        top = jnp.max(x, axis=0, keepdims=True)
        tot = jnp.sum(jnp.exp(x - top), axis=0, keepdims=True)
        csend[it, 0:1, :] = top
        csend[it, 1:2, :] = tot
        rows_swap(it)
        if it == 1:
            gather_round(0, 3)
        if it == 2:
            gather_round(0, 4)
        await_all(crecv.at[it], cr.at[it])
        g = merge(crecv[it], top, tot)

        x = g - a_ref[...]
        top = jnp.max(x, axis=1, keepdims=True)
        tot = jnp.sum(jnp.exp(x - top), axis=1, keepdims=True)
        top, tot = flat(top, tot)
        rsend[it, 0:1, :] = top
        rsend[it, 1:2, :] = tot
        cols_swap(it)
        if it == 1:
            gather_round(1, 2)
        await_all(rrecv.at[it], rr.at[it])
        f = tall(merge(rrecv[it], top, tot), n)
    p_ref[...] = (float(tokens) * jnp.exp(f + g - a_ref[...])).astype(BF16)
    for it in range(ITERS):
        await_all(crecv.at[it], cs.at[it])
        await_all(rrecv.at[it], rs.at[it])

    def at_x(d, k):
        return (row, ring(xx + d) * 2 + k)

    def cols_reduce(make, t):
        def copy(i, src, dst, to):
            return rcopy(src, dst, xs.at[t, i], xr.at[t, i], to)

        twin = []
        for i, d in enumerate(ORDER):
            sibs[i] = make(ring(xx + d) * 2 + 1 - core).astype(BF16)
            twin.append(copy(i, sibs.at[i], sibr.at[i], at_x(0, 1 - core)))

        def both(i, d):
            value = make(ring(xx + d) * 2 + core)
            twin[i].wait_recv()
            return value + sibr[i].astype(F32)

        xo[...] = both(0, 2).astype(BF16)
        c4 = copy(4, xo.at[0:hn], rh.at[0], at_x(1, core))
        c5 = copy(5, xo.at[hn:n], rh.at[1], at_x(-1, core))
        xp[...] = both(1, 1).astype(BF16)
        c6 = copy(6, xp.at[hn:n], rf.at[0, hn:n], at_x(1, core))
        xm[...] = both(2, 3).astype(BF16)
        c7 = copy(7, xm.at[0:hn], rf.at[1, 0:hn], at_x(-1, core))
        own[...] = both(3, 0)
        c4.wait_recv()
        xp[0:hn] = (xp[0:hn].astype(F32) + rh[0].astype(F32)).astype(BF16)
        c8 = copy(8, xp.at[0:hn], rf.at[0, 0:hn], at_x(1, core))
        c5.wait_recv()
        xm[hn:n] = (xm[hn:n].astype(F32) + rh[1].astype(F32)).astype(BF16)
        c9 = copy(9, xm.at[hn:n], rf.at[1, hn:n], at_x(-1, core))
        for c in (c6, c7, c8, c9):
            c.wait_recv()
        for c in twin + [c4, c5, c6, c7, c8, c9]:
            c.wait_send()
        return own[...] + rf[0].astype(F32) + rf[1].astype(F32)

    def cols_gather(ref, t, use):
        me = col

        def slot(d, k):
            return ring(xx + d) * 2 + k

        def copy(i, src, to):
            return rcopy(src, src, ug_s.at[t, i], ug_r.at[t, i], to)

        other = 1 - core
        lo, hi = pl.ds(0, hn), pl.ds(hn, hn)
        twin = at_x(0, other)
        c0 = copy(0, ref.at[me], at_x(1, core))
        c1 = copy(1, ref.at[me], at_x(-1, core))
        c2 = copy(2, ref.at[me], twin)
        use(me, True)
        c2.wait_recv()
        use(slot(0, other), False)
        c0.wait_recv()
        c3 = copy(3, ref.at[slot(-1, core), lo], at_x(1, core))
        c5 = copy(5, ref.at[slot(-1, core)], twin)
        c1.wait_recv()
        c4 = copy(4, ref.at[slot(1, core), hi], at_x(-1, core))
        c6 = copy(6, ref.at[slot(1, core)], twin)
        use(slot(-1, core), False)
        use(slot(1, core), False)
        c3.wait_recv()
        c7 = copy(7, ref.at[slot(2, core), lo], twin)
        c4.wait_recv()
        c8 = copy(8, ref.at[slot(2, core), hi], twin)
        c5.wait_recv()
        use(slot(-1, other), False)
        c6.wait_recv()
        use(slot(1, other), False)
        use(slot(2, core), False)
        c7.wait_recv()
        c8.wait_recv()
        use(slot(2, other), False)
        for c in (c0, c1, c2, c3, c4, c5, c6, c7, c8):
            c.wait_send()

    gather_round(1, 3)

    def target_block(fb):
        rows_at = pl.ds(pl.multiple_of(fb // 2 * m, m), m)
        lanes = pl.ds(pl.multiple_of(lax.rem(fb, 2) * share, share), share)
        return jnp.dot(p_ref[...], dbuf[rows_at, lanes], preferred_element_type=F32)

    target_ref[...] = cols_reduce(target_block, 0).astype(BF16)
    target = target_ref[...].astype(F32)
    noise = slopes[col].astype(F32)
    t = tall(times_ref[...], n)
    lanes = pl.ds(pl.multiple_of(col * share, share), share)
    st = (1.0 - t) * noise + t * target + t * embed_ref[:, lanes]
    latents[col] = (st * gain_ref[:, lanes]).astype(BF16)
    state[...] = st - (target - noise)
    part = jnp.sum(st * st, axis=1, keepdims=True)
    part, _ = flat(part, part)
    rsend[ITERS, 0:1, :] = part
    rsend[ITERS, 1:2, :] = part
    cols_swap(ITERS)

    tiles = ffd // 256

    def tile(j):
        return pl.ds(pl.multiple_of(j * 256, 256), 256)

    def block(i):
        return pl.ds(pl.multiple_of(i * share, share), share)

    gather_round(0, 5)

    def use_latent(i, first):
        def step(j, _):
            value = jnp.dot(latents[i], win[block(i), tile(j)], preferred_element_type=F32)
            hid[:, tile(j)] = value if first else hid[:, tile(j)] + value
            return 0

        lax.fori_loop(0, tiles, step, 0)

    cols_gather(latents, 0, use_latent)
    gather_round(1, 4)
    await_all(rrecv.at[ITERS], rr.at[ITERS])
    await_all(rrecv.at[ITERS], rs.at[ITERS])
    square = part + jnp.sum(rrecv[ITERS][:, 0, :], axis=0, keepdims=True)
    scale = tall(lax.rsqrt(square / width + 1e-6), n)

    def gelu_step(j, _):
        h = hid[:, tile(j)] * scale
        c = math.sqrt(2.0 / math.pi)
        h2 = h * h
        th = jnp.tanh(c * (h + 0.044715 * (h2 * h)))
        act[:, tile(j)] = (0.5 * h * (1.0 + th)).astype(BF16)
        slope_of = 0.5 * (1.0 + th) + 0.5 * h * (1.0 - th * th) * (c * (1.0 + (3 * 0.044715) * h2))
        hid[:, tile(j)] = slope_of * scale
        return 0

    lax.fori_loop(0, tiles, gelu_step, 0)
    gather_round(1, 5)

    def velocity_block(fb):
        return lax.dot_general(act[...], wout[block(fb), :], NT, preferred_element_type=F32)

    slopes[col] = ((state[...] + cols_reduce(velocity_block, 1)) * (1.0 / math.sqrt(tokens))).astype(BF16)

    def use_slope(i, _):
        turned[...] = slopes[i].astype(F32).T.astype(BF16)

        def step(j, _):
            dbuf[block(i), tile(j)] = jnp.dot(turned[...], act[:, tile(j)], preferred_element_type=F32).astype(BF16)
            return 0

        lax.fori_loop(0, tiles, step, 0)

    cols_gather(slopes, 1, use_slope)

    def rx_at(ref, path, j, part=None):
        off = qw if part == 1 else 0
        size = hw if part is None else qw
        return ref.at[pl.ds((path * 16 + j) * hw + off, size)]

    scatters = {}

    def scatter(w, step):
        ref = (dbuf, win)[w]
        land = (rx, wout)[w]

        def copy(path, i, src, dst, axis, d):
            scatters[w, path, i] = rcopy(src, dst, gr_s.at[w, path, i], gr_r.at[w, path, i], toward(path, axis, d))

        def got(path, i):
            scatters[w, path, i].wait_recv()

        def add(at, *more):
            value = at[...].astype(F32)
            for r in more:
                value = value + r[...].astype(F32)
            at[...] = value.astype(BF16)

        for path in range(2):
            f, s = here(path)
            if step == 1:
                for j, e in enumerate((2, 1)):
                    copy(path, j, piece(ref, path, f + 2, s + e), rx_at(land, path, j), "f", 1)
                for j, e in enumerate((3, 0)):
                    copy(path, 2 + j, piece(ref, path, f + 2, s + e), rx_at(land, path, 2 + j), "f", -1)
                for e in (3, 0):
                    copy(path, 4 + e, piece(ref, path, f + 1, s + e), rx_at(land, path, 4 + e), "f", 1)
                for e in (2, 1):
                    copy(path, 8 + e, piece(ref, path, f - 1, s + e), rx_at(land, path, 8 + e), "f", -1)
            if step == 2:
                for j in range(2):
                    e = (2, 1)[j]
                    got(path, j)
                    at = piece(ref, path, f + 1, s + e)
                    add(at, rx_at(land, path, j))
                    copy(path, 4 + e, at, rx_at(land, path, 4 + e), "f", 1)
                    e = (3, 0)[j]
                    got(path, 2 + j)
                    at = piece(ref, path, f - 1, s + e)
                    add(at, rx_at(land, path, 2 + j))
                    copy(path, 8 + e, at, rx_at(land, path, 8 + e), "f", -1)
            if step == 3:
                for e in ORDER:
                    got(path, 4 + e)
                    got(path, 8 + e)
                    add(piece(ref, path, f, s + e), rx_at(land, path, 4 + e), rx_at(land, path, 8 + e))
                    if e == 2:
                        copy(path, 12, piece(ref, path, f, s + 2, 0), rx_at(land, path, 12, 0), "s", 1)
                        copy(path, 13, piece(ref, path, f, s + 2, 1), rx_at(land, path, 12, 1), "s", -1)
                    if e == 1:
                        copy(path, 14, piece(ref, path, f, s + 1, 1), rx_at(land, path, 13, 1), "s", 1)
                    if e == 3:
                        copy(path, 15, piece(ref, path, f, s - 1, 0), rx_at(land, path, 14, 0), "s", -1)
            if step == 4:
                got(path, 12)
                at = piece(ref, path, f, s + 1, 0)
                add(at, rx_at(land, path, 12, 0))
                copy(path, 16, at, rx_at(land, path, 13, 0), "s", 1)
                got(path, 13)
                at = piece(ref, path, f, s - 1, 1)
                add(at, rx_at(land, path, 12, 1))
                copy(path, 17, at, rx_at(land, path, 14, 1), "s", -1)
            if step == 5:
                for i in range(14, 18):
                    got(path, i)
                value = (piece(ref, path, f, s)[...].astype(F32) + rx_at(land, path, 13)[...].astype(F32)
                         + rx_at(land, path, 14)[...].astype(F32))
                half = slice(path * hw, (path + 1) * hw)
                if w == 0:
                    gout_ref[:, half] = value.T.astype(BF16)
                else:
                    gin_ref[half, :] = value.astype(BF16)
                for i in range(18):
                    scatters[w, path, i].wait_send()

    scatter(0, 1)

    back[...] = jnp.zeros_like(back)

    def back_step(i, _):
        def step(j, _):
            back[:, tile(j)] += jnp.dot(slopes[i], wout[block(i), tile(j)], preferred_element_type=F32)
            return 0

        return lax.fori_loop(0, tiles, step, 0)

    lax.fori_loop(0, n_cols, back_step, 0)
    for c in gathers.values():
        c.wait_send()
    for path in range(2):
        for d in (1, -1):
            pl.semaphore_signal(credit, inc=1, device_id=toward(path, "f", d), device_id_type=MESH)
    scatter(0, 2)
    sh[...] = (back[...] * hid[...]).astype(BF16)

    def in_step(i, _):
        turned[...] = latents[i].astype(F32).T.astype(BF16)

        def step(j, _):
            win[block(i), tile(j)] = jnp.dot(turned[...], sh[:, tile(j)], preferred_element_type=F32).astype(BF16)
            return 0

        return lax.fori_loop(0, tiles, step, 0)

    lax.fori_loop(0, n_cols, in_step, 0)
    pl.semaphore_wait(credit, 4)
    scatter(1, 1)
    scatter(0, 3)
    scatter(1, 2)
    scatter(0, 4)
    scatter(0, 5)
    scatter(1, 3)
    scatter(1, 4)
    scatter(1, 5)


def per_device(noise, data, times, time_embed, norm_gain, w_in, w_out):
    n, width = noise.shape
    m = data.shape[0]
    wr, ffd = w_in.shape
    share = width // 8
    vm = pl.BlockSpec(memory_space=pltpu.VMEM)
    hbm = pl.BlockSpec(memory_space=pl.ANY)
    dma = pltpu.SemaphoreType.DMA
    return pl.pallas_call(
        kernel,
        out_shape=(
            jax.ShapeDtypeStruct((n, share), BF16),
            jax.ShapeDtypeStruct((wr, ffd), BF16),
            jax.ShapeDtypeStruct((ffd, wr), BF16),
        ),
        in_specs=[hbm, hbm, vm, vm, vm, hbm, vm],
        out_specs=(vm, vm, vm),
        scratch_shapes=[
            pltpu.VMEM((8, n, share), BF16),
            pltpu.VMEM((width, ffd), BF16),
            pltpu.VMEM((width, ffd), BF16),
            pltpu.VMEM((width, ffd), BF16),
            pltpu.VMEM((width, ffd), BF16),
            pltpu.VMEM((8, n, share), BF16),
            pltpu.VMEM((n, ffd), BF16),
            pltpu.VMEM((n, ffd), F32),
            pltpu.VMEM((n, ffd), F32),
            pltpu.VMEM((n, m), F32),
            pltpu.VMEM((n, m), BF16),
            pltpu.VMEM((n, share), F32),
            pltpu.VMEM((n, ffd), BF16),
            pltpu.VMEM((share, n), BF16),
            pltpu.VMEM((4, n, share), BF16),
            pltpu.VMEM((4, n, share), BF16),
            pltpu.VMEM((n, share), BF16),
            pltpu.VMEM((n, share), BF16),
            pltpu.VMEM((n, share), BF16),
            pltpu.VMEM((2, n // 2, share), BF16),
            pltpu.VMEM((2, n, share), BF16),
            pltpu.VMEM((n, share), F32),
            pltpu.VMEM((ITERS, 2, m), F32),
            pltpu.VMEM((ITERS, 15, 2, m), F32),
            pltpu.VMEM((ITERS + 1, 2, n), F32),
            pltpu.VMEM((ITERS + 1, 7, 2, n), F32),
            dma((ITERS,)), dma((ITERS,)), dma((ITERS + 1,)), dma((ITERS + 1,)),
            dma((2, 2, 20)), dma((2, 2, 20)),
            dma((2, 10)), dma((2, 10)),
            dma((2, 9)), dma((2, 9)),
            dma((2, 2, 18)), dma((2, 2, 18)),
            dma((13,)),
            pltpu.SemaphoreType.REGULAR,
        ],
        compiler_params=pltpu.CompilerParams(
            collective_id=0, has_side_effects=True, vmem_limit_bytes=62 * 2**20
        ),
    )(noise, data, times[None, :], time_embed[None, :], norm_gain[None, :], w_in, w_out)


def solution(mesh):
    in_specs = (
        P("rows", None),
        P("cols", None),
        P("rows"),
        P(),
        P(),
        P("rows", "cols"),
        P("cols", "rows"),
    )
    out_specs = (P("rows", "cols"), P("rows", "cols"), P("cols", "rows"))
    return jax.shard_map(
        per_device, mesh=mesh, in_specs=in_specs, out_specs=out_specs, check_vma=False
    )
```

```python
import functools
import math

import jax
import jax.numpy as jnp
from jax import lax
from jax.experimental import pallas as pl
from jax.experimental.pallas import tpu as pltpu
from jax.sharding import PartitionSpec as P

ITERS = 3
EPSILON = 0.01
MESH = pl.DeviceIdType.MESH
F32 = jnp.float32
BF16 = jnp.bfloat16
NT = (((1,), (1,)), ((), ()))
ORDER = (2, 1, 3, 0)


def ring(value):
    return lax.rem(value + 4, 4)


def tall(row, rows):
    return jnp.broadcast_to(row, (128, rows)).T[:, 0:1]


def flat(left, right):
    lane = lax.broadcasted_iota(jnp.int32, (left.shape[0], 128), 1)
    both = jnp.where(lane < 64, left, right).T
    return both[0:1], both[64:65]


def kernel(noise_hbm, data_hbm, times_ref, embed_ref, gain_ref, w_in_hbm, w_out_ref,
           target_ref, gin_ref, gout_ref,
           slopes, dbuf, win, wout, rx, latents, act, hid, back, a_ref, p_ref, state, sh, turned,
           sibs, sibr, xo, xp, xm, rh, rf, own, nsq, dsq, final,
           csend, crecv, rsend, rrecv,
           cs, cr, rs, rr, ag_s, ag_r, xs, xr, ug_s, ug_r, gr_s, gr_r, loc, credit):
    n_rows, n_cols = 16, 8
    row = lax.axis_index("rows")
    col = lax.axis_index("cols")
    z, y = row // 4, lax.rem(row, 4)
    xx, core = col // 2, lax.rem(col, 2)
    n, width = noise_hbm.shape
    m = data_hbm.shape[0]
    share = width // n_cols
    wr, ffd = w_in_hbm.shape
    half = share // 2
    eighth = share // 4
    hn = n // 2
    tokens = n * n_rows

    def rcopy(src, dst, send, recv, to):
        c = pltpu.make_async_remote_copy(src_ref=src, dst_ref=dst, send_sem=send, recv_sem=recv,
                                         device_id=to, device_id_type=MESH)
        c.start()
        return c

    barrier = pltpu.get_barrier_semaphore()
    for d in range(1, n_rows):
        pl.semaphore_signal(barrier, inc=1, device_id=(lax.rem(row + d, n_rows), col), device_id_type=MESH)
    for d in range(1, n_cols):
        pl.semaphore_signal(barrier, inc=1, device_id=(row, lax.rem(col + d, n_cols)), device_id_type=MESH)

    def mine(i):
        return pl.ds(pl.multiple_of(i * wr, wr), wr)

    w_copy = pltpu.make_async_copy(w_in_hbm, win.at[mine(row)], loc.at[0])
    w_copy.start()

    def noise_copy(q):
        return pltpu.make_async_copy(noise_hbm.at[:, pl.ds(pl.multiple_of(q * half, half), half)],
                                     slopes.at[lax.rem(q, 2), q // 2], loc.at[5 + q])

    def data_copy(q):
        return pltpu.make_async_copy(data_hbm.at[:, pl.ds(pl.multiple_of(q * 2 * share, 2 * share), 2 * share)],
                                     dbuf.at[pl.ds(pl.multiple_of(q * m, m), m)], loc.at[1 + q])

    for q in range(4):
        for h in range(4):
            noise_copy(4 * q + h).start()
        data_copy(q).start()
    wout[mine(row)] = w_out_ref[...].astype(F32).T.astype(BF16)
    w_copy.wait()

    def place(path, f, s):
        return s * 4 + f if path == 0 else f * 4 + s

    def here(path):
        return (y, z) if path == 0 else (z, y)

    def piece(ref, unit, path, f, s, part=None):
        base, high = unit
        off = base + path * high + (high // 2 if part == 1 else 0)
        size = high if part is None else high // 2
        return ref.at[pl.ds(pl.multiple_of(place(path, ring(f), ring(s)) * wr + off, high // 2), size)]

    wide, low, up = (0, wr // 2), (0, wr // 4), (wr // 2, wr // 4)

    def toward(path, axis, d):
        f, s = here(path)
        if axis == "f":
            return (place(path, ring(f + d), s), col)
        return (place(path, f, ring(s + d)), col)

    gathers = {}

    def gather(w, *steps):
        ref = (win, wout, wout)[w]
        unit = (wide, low, up)[w]
        jobs = {
            "1": [(0, "f", 1, 0, 0, None), (1, "f", -1, 0, 0, None), (2, "s", 1, 0, 0, None), (3, "s", -1, 0, 0, None)],
            "2a": [(4, "f", 1, -1, 0, 0), (5, "f", -1, 1, 0, 1),
                   (6, "s", 1, -1, 0, None), (7, "s", -1, -1, 0, None), (8, "s", 1, 1, 0, None), (9, "s", -1, 1, 0, None)],
            "2b": [(10, "s", 1, 0, -1, 0), (11, "s", -1, 0, 1, 1)],
            "3a": [(12, "s", 1, 2, 0, None), (13, "s", -1, 2, 0, None)],
            "3b": [(14, "s", 1, -1, -1, 0), (15, "s", -1, -1, 1, 1)],
            "3c": [(16, "s", 1, 1, -1, 0), (17, "s", -1, 1, 1, 1)],
            "4": [(18, "s", 1, 2, -1, 0), (19, "s", -1, 2, 1, 1)],
        }
        needs = {"2a": (0, 1), "2b": (2, 3), "3a": (4, 5), "3b": (6, 7), "3c": (8, 9), "4": (12, 13),
                 "end": (10, 11, 14, 15, 16, 17, 18, 19)}
        for step in steps:
            for i in needs.get(step, ()):
                for path in range(2):
                    gathers[w, path, i].wait_recv()
            for i, axis, d, df, ds_, part in jobs.get(step, ()):
                for path in range(2):
                    f, s = here(path)
                    at = piece(ref, unit, path, f + df, s + ds_, part)
                    gathers[w, path, i] = rcopy(at, at, ag_s.at[w, path, i], ag_r.at[w, path, i], toward(path, axis, d))

    pl.semaphore_wait(barrier, n_rows + n_cols - 2)
    gather(0, "1")
    gather(1, "1")

    def squares(value):
        value = value.astype(F32)
        value = value * value
        out = value[:, 0:128]
        for j in range(1, value.shape[1] // 128):
            out = out + value[:, j * 128 : (j + 1) * 128]
        return out

    for q in range(4):
        for h in range(4):
            noise_copy(4 * q + h).wait()
        data_copy(q).wait()
        total = None
        for h in range(4):
            term = lax.dot_general(slopes[h % 2, 2 * q + h // 2],
                                   dbuf[q * m : (q + 1) * m, h * half : (h + 1) * half], NT,
                                   preferred_element_type=F32)
            total = term if total is None else total + term
        a_ref[...] = total if q == 0 else a_ref[...] + total

        def noise_rows(i, _, q=q):
            at = pl.ds(pl.multiple_of(i * 32, 32), 32)
            value = squares(slopes[0, 2 * q, at, :])
            for h in range(1, 4):
                value = value + squares(slopes[h % 2, 2 * q + h // 2, at, :])
            nsq[at, :] = value if q == 0 else nsq[at, :] + value
            return 0

        def data_rows(i, _, q=q):
            at = pl.ds(pl.multiple_of(i * 32, 32), 32)
            value = squares(dbuf[pl.ds(pl.multiple_of(q * m + i * 32, 32), 32), :])
            dsq[at, :] = value if q == 0 else dsq[at, :] + value
            return 0

        lax.fori_loop(0, n // 32, noise_rows, 0)
        lax.fori_loop(0, m // 32, data_rows, 0)
    noise_sq = jnp.sum(nsq[...], axis=1, keepdims=True)
    data_sq = jnp.sum(dsq[...].T, axis=0, keepdims=True)
    a_ref[...] = (noise_sq + data_sq - 2.0 * a_ref[...]) * (1.0 / (width * EPSILON))
    base = -math.log(tokens)
    gather(0, "2a", "2b")

    def rows_swap(it):
        for d in range(1, n_rows):
            rcopy(csend.at[it], crecv.at[it, d - 1], cs.at[it], cr.at[it], (lax.rem(row + d, n_rows), col))

    def cols_swap(it):
        for d in range(1, n_cols):
            rcopy(rsend.at[it], rrecv.at[it, d - 1], rs.at[it], rr.at[it], (row, lax.rem(col + d, n_cols)))

    def await_all(ref, sem):
        pltpu.make_async_copy(ref, ref, sem).wait()

    def merge(got, top, tot):
        gt = got[:, 0, :]
        best = jnp.maximum(top, jnp.max(gt, axis=0, keepdims=True))
        total = tot * jnp.exp(top - best) + jnp.sum(got[:, 1, :] * jnp.exp(gt - best), axis=0, keepdims=True)
        return base - (best + jnp.log(total))

    f = jnp.zeros((n, 1), F32)
    g = None
    for it in range(ITERS):
        x = f - a_ref[...]
        top = jnp.max(x, axis=0, keepdims=True)
        tot = jnp.sum(jnp.exp(x - top), axis=0, keepdims=True)
        csend[it, 0:1, :] = top
        csend[it, 1:2, :] = tot
        rows_swap(it)
        if it == 2:
            gather(0, "3a", "3b", "3c")
            gather(1, "2a", "2b")
        await_all(crecv.at[it], cr.at[it])
        g = merge(crecv[it], top, tot)

        x = g - a_ref[...]
        top = jnp.max(x, axis=1, keepdims=True)
        tot = jnp.sum(jnp.exp(x - top), axis=1, keepdims=True)
        top, tot = flat(top, tot)
        rsend[it, 0:1, :] = top
        rsend[it, 1:2, :] = tot
        cols_swap(it)
        if it == 0:
            gather(2, "1")
        await_all(rrecv.at[it], rr.at[it])
        f = tall(merge(rrecv[it], top, tot), n)
    p_ref[...] = (float(tokens) * jnp.exp(f + g - a_ref[...])).astype(BF16)
    for it in range(ITERS):
        await_all(crecv.at[it], cs.at[it])
        await_all(rrecv.at[it], rs.at[it])

    def at_x(d, k):
        return (row, ring(xx + d) * 2 + k)

    def cols_reduce(make, t, u):
        def copy(i, src, dst, to):
            return rcopy(src, dst, xs.at[t, u, i], xr.at[t, u, i], to)

        c = {}

        def begin():
            for i, d in enumerate(ORDER):
                sibs[u, i] = make(ring(xx + d) * 2 + 1 - core, u).astype(BF16)
                c[i] = copy(i, sibs.at[u, i], sibr.at[u, i], at_x(0, 1 - core))
                value = make(ring(xx + d) * 2 + core, u)
                c[i].wait_recv()
                value = value + sibr[u, i].astype(F32)
                if d == 0:
                    own[u] = value
                    continue
                out = (xo, xp, None, xm)[i if i < 2 else 3]
                out[u] = value.astype(BF16)
                if d == 2:
                    c[4] = copy(4, out.at[u, 0:hn], rh.at[u, 0], at_x(1, core))
                    c[5] = copy(5, out.at[u, hn:n], rh.at[u, 1], at_x(-1, core))
                elif d == 1:
                    c[6] = copy(6, out.at[u, hn:n], rf.at[u, 0, hn:n], at_x(1, core))
                else:
                    c[7] = copy(7, out.at[u, 0:hn], rf.at[u, 1, 0:hn], at_x(-1, core))

        def middle():
            c[4].wait_recv()
            xp[u, 0:hn] = (xp[u, 0:hn].astype(F32) + rh[u, 0].astype(F32)).astype(BF16)
            c[8] = copy(8, xp.at[u, 0:hn], rf.at[u, 0, 0:hn], at_x(1, core))
            c[5].wait_recv()
            xm[u, hn:n] = (xm[u, hn:n].astype(F32) + rh[u, 1].astype(F32)).astype(BF16)
            c[9] = copy(9, xm.at[u, hn:n], rf.at[u, 1, hn:n], at_x(-1, core))

        def finish():
            for i in (6, 7, 8, 9):
                c[i].wait_recv()
            value = own[u] + rf[u, 0].astype(F32) + rf[u, 1].astype(F32)
            for i in range(10):
                c[i].wait_send()
            return value

        return begin, middle, finish

    def slot(d, k):
        return ring(xx + d) * 2 + k

    other = 1 - core

    def cols_gather(ref, t, u):
        def copy(i, src, to):
            return rcopy(src, src, ug_s.at[t, u, i], ug_r.at[t, u, i], to)

        lo, hi = pl.ds(0, hn), pl.ds(hn, hn)
        twin = at_x(0, other)
        c = {}

        def begin():
            c[0] = copy(0, ref.at[u, col], at_x(1, core))
            c[1] = copy(1, ref.at[u, col], at_x(-1, core))
            c[2] = copy(2, ref.at[u, col], twin)

        def middle():
            c[0].wait_recv()
            c[3] = copy(3, ref.at[u, slot(-1, core), lo], at_x(1, core))
            c[5] = copy(5, ref.at[u, slot(-1, core)], twin)
            c[1].wait_recv()
            c[4] = copy(4, ref.at[u, slot(1, core), hi], at_x(-1, core))
            c[6] = copy(6, ref.at[u, slot(1, core)], twin)

        def finish():
            c[3].wait_recv()
            c[7] = copy(7, ref.at[u, slot(2, core), lo], twin)
            c[4].wait_recv()
            c[8] = copy(8, ref.at[u, slot(2, core), hi], twin)

        def got(*which):
            for i in which:
                c[i].wait_recv()

        def close():
            for i in range(9):
                c[i].wait_send()

        return begin, middle, finish, got, close

    tiles = ffd // 256

    def tile(j):
        return pl.ds(pl.multiple_of(j * 256, 256), 256)

    def rows_of(i, u, size):
        return pl.ds(pl.multiple_of(i * share + u * size, size), size)

    def target_block(fb, u):
        rows_at = pl.ds(pl.multiple_of(fb // 2 * m, m), m)
        lanes = pl.ds(pl.multiple_of(lax.rem(fb, 2) * share + u * half, half), half)
        return jnp.dot(p_ref[...], dbuf[rows_at, lanes], preferred_element_type=F32)

    t = tall(times_ref[...][None, :], n)

    def make_state(value, u):
        target = value.astype(BF16)
        target_ref[:, u * half : (u + 1) * half] = target
        target = target.astype(F32)
        noise = slopes[u, col].astype(F32)
        lanes = pl.ds(pl.multiple_of(col * share + u * half, half), half)
        st = (1.0 - t) * noise + t * target + t * embed_ref[:, lanes]
        latents[u, col] = (st * gain_ref[:, lanes]).astype(BF16)
        state[:, u * half : (u + 1) * half] = st - (target - noise)
        return jnp.sum(st * st, axis=1, keepdims=True)

    begin0, middle0, finish0 = cols_reduce(target_block, 0, 0)
    begin1, middle1, finish1 = cols_reduce(target_block, 0, 1)
    hb0, hm0, hf0, hg0, hc0 = cols_gather(latents, 0, 0)
    hb1, hm1, hf1, hg1, hc1 = cols_gather(latents, 0, 1)
    begin0()
    middle0()
    begin1()
    middle1()
    gather(0, "4")
    part = make_state(finish0(), 0)
    hb0()
    part = part + make_state(finish1(), 1)
    part, _ = flat(part, part)
    rsend[ITERS, 0:1, :] = part
    rsend[ITERS, 1:2, :] = part
    cols_swap(ITERS)
    hm0()
    hb1()
    gather(2, "2a", "2b")
    gather(0, "end")

    def use_latent(i, first=False):
        def step(j, _):
            value = (jnp.dot(latents[0, i], win[rows_of(i, 0, half), tile(j)], preferred_element_type=F32)
                     + jnp.dot(latents[1, i], win[rows_of(i, 1, half), tile(j)], preferred_element_type=F32))
            hid[:, tile(j)] = value if first else hid[:, tile(j)] + value
            return 0

        lax.fori_loop(0, tiles, step, 0)

    use_latent(col, True)
    gather(1, "3a", "3b", "3c")
    hf0()
    hm1()
    hg0(2)
    hg1(2)
    use_latent(slot(0, other))
    use_latent(slot(-1, core))
    hf1()
    use_latent(slot(1, core))
    gather(1, "4")
    hg0(5)
    hg1(5)
    use_latent(slot(-1, other))
    hg0(6)
    hg1(6)
    use_latent(slot(1, other))
    use_latent(slot(2, core))
    gather(2, "3a", "3b", "3c")
    hg0(7, 8)
    hg1(7, 8)
    use_latent(slot(2, other))
    hc0()
    hc1()
    await_all(rrecv.at[ITERS], rr.at[ITERS])
    await_all(rrecv.at[ITERS], rs.at[ITERS])
    square = part + jnp.sum(rrecv[ITERS][:, 0, :], axis=0, keepdims=True)
    scale = tall(lax.rsqrt(square / width + 1e-6), n)

    def gelu_step(j, _):
        h = hid[:, tile(j)] * scale
        c = math.sqrt(2.0 / math.pi)
        h2 = h * h
        th = jnp.tanh(c * (h + 0.044715 * (h2 * h)))
        act[:, tile(j)] = (0.5 * h * (1.0 + th)).astype(BF16)
        slope_of = 0.5 * (1.0 + th) + 0.5 * h * (1.0 - th * th) * (c * (1.0 + (3 * 0.044715) * h2))
        hid[:, tile(j)] = slope_of * scale
        return 0

    lax.fori_loop(0, tiles, gelu_step, 0)
    gather(1, "end")

    def pair(ref, i, u, at):
        lo = ref[pl.ds(pl.multiple_of(i * share + u * eighth, eighth), eighth), at]
        hi = ref[pl.ds(pl.multiple_of(i * share + half + u * eighth, eighth), eighth), at]
        return jnp.concatenate([lo, hi], axis=0)

    def velocity_block(fb, u):
        return lax.dot_general(act[...], pair(wout, fb, u, slice(None)), NT, preferred_element_type=F32)

    def make_slope(value, u):
        lo = state[:, u * eighth : (u + 1) * eighth]
        hi = state[:, half + u * eighth : half + (u + 1) * eighth]
        slopes[u, col] = ((jnp.concatenate([lo, hi], axis=1) + value) * (1.0 / math.sqrt(tokens))).astype(BF16)

    def use_slope(i, u):
        turned[...] = slopes[u, i].astype(F32).T.astype(BF16)

        def step(j, _):
            value = jnp.dot(turned[...], act[:, tile(j)], preferred_element_type=F32).astype(BF16)
            dbuf[pl.ds(pl.multiple_of(i * share + u * eighth, eighth), eighth), tile(j)] = value[:eighth]
            dbuf[pl.ds(pl.multiple_of(i * share + half + u * eighth, eighth), eighth), tile(j)] = value[eighth:]
            return 0

        lax.fori_loop(0, tiles, step, 0)

    def rx_at(ref, base, unit, path, j, part=None):
        high = unit[1]
        off = high // 2 if part == 1 else 0
        size = high if part is None else high // 2
        return ref.at[pl.ds(base + (path * 16 + j) * high + off, size)]

    scatters = {}

    def scatter(w, step):
        ref = (dbuf, dbuf, win)[w]
        unit = (low, up, wide)[w]
        land = (rx, rx, wout)[w]
        base = (0, width // 2, 0)[w]
        high = unit[1]

        def copy(path, i, src, dst, axis, d):
            scatters[w, path, i] = rcopy(src, dst, gr_s.at[w, path, i], gr_r.at[w, path, i], toward(path, axis, d))

        def got(path, i):
            scatters[w, path, i].wait_recv()

        def add(at, *more):
            value = at[...].astype(F32)
            for r in more:
                value = value + r[...].astype(F32)
            at[...] = value.astype(BF16)

        for path in range(2):
            f, s = here(path)
            if step == 1:
                for j, e in enumerate((2, 1)):
                    copy(path, j, piece(ref, unit, path, f + 2, s + e), rx_at(land, base, unit, path, j), "f", 1)
                for j, e in enumerate((3, 0)):
                    copy(path, 2 + j, piece(ref, unit, path, f + 2, s + e), rx_at(land, base, unit, path, 2 + j), "f", -1)
                for e in (3, 0):
                    copy(path, 4 + e, piece(ref, unit, path, f + 1, s + e), rx_at(land, base, unit, path, 4 + e), "f", 1)
                for e in (2, 1):
                    copy(path, 8 + e, piece(ref, unit, path, f - 1, s + e), rx_at(land, base, unit, path, 8 + e), "f", -1)
            if step == 2:
                for j in range(2):
                    e = (2, 1)[j]
                    got(path, j)
                    at = piece(ref, unit, path, f + 1, s + e)
                    add(at, rx_at(land, base, unit, path, j))
                    copy(path, 4 + e, at, rx_at(land, base, unit, path, 4 + e), "f", 1)
                    e = (3, 0)[j]
                    got(path, 2 + j)
                    at = piece(ref, unit, path, f - 1, s + e)
                    add(at, rx_at(land, base, unit, path, 2 + j))
                    copy(path, 8 + e, at, rx_at(land, base, unit, path, 8 + e), "f", -1)
            if step == 3:
                for e in ORDER:
                    got(path, 4 + e)
                    got(path, 8 + e)
                    add(piece(ref, unit, path, f, s + e), rx_at(land, base, unit, path, 4 + e), rx_at(land, base, unit, path, 8 + e))
                    if e == 2:
                        copy(path, 12, piece(ref, unit, path, f, s + 2, 0), rx_at(land, base, unit, path, 12, 0), "s", 1)
                        copy(path, 13, piece(ref, unit, path, f, s + 2, 1), rx_at(land, base, unit, path, 12, 1), "s", -1)
                    if e == 1:
                        copy(path, 14, piece(ref, unit, path, f, s + 1, 1), rx_at(land, base, unit, path, 13, 1), "s", 1)
                    if e == 3:
                        copy(path, 15, piece(ref, unit, path, f, s - 1, 0), rx_at(land, base, unit, path, 14, 0), "s", -1)
            if step == 4:
                got(path, 12)
                at = piece(ref, unit, path, f, s + 1, 0)
                add(at, rx_at(land, base, unit, path, 12, 0))
                copy(path, 16, at, rx_at(land, base, unit, path, 13, 0), "s", 1)
                got(path, 13)
                at = piece(ref, unit, path, f, s - 1, 1)
                add(at, rx_at(land, base, unit, path, 12, 1))
                copy(path, 17, at, rx_at(land, base, unit, path, 14, 1), "s", -1)
            if step == 5:
                for i in range(14, 18):
                    got(path, i)
                value = (piece(ref, unit, path, f, s)[...].astype(F32) + rx_at(land, base, unit, path, 13)[...].astype(F32)
                         + rx_at(land, base, unit, path, 14)[...].astype(F32))
                if w < 2:
                    final[w, path * high : (path + 1) * high, :] = value
                    if path == 1:
                        gout_ref[:, w * 2 * high : (w + 1) * 2 * high] = final[w].T.astype(BF16)
                else:
                    gin_ref[path * high : (path + 1) * high, :] = value.astype(BF16)
                for i in range(18):
                    scatters[w, path, i].wait_send()

    begin0, middle0, finish0 = cols_reduce(velocity_block, 1, 0)
    begin1, middle1, finish1 = cols_reduce(velocity_block, 1, 1)
    sb0, sm0, sf0, sg0, sc0 = cols_gather(slopes, 1, 0)
    sb1, sm1, sf1, sg1, sc1 = cols_gather(slopes, 1, 1)
    begin0()
    middle0()
    gather(2, "4", "end")
    begin1()
    middle1()
    make_slope(finish0(), 0)
    sb0()
    use_slope(col, 0)
    make_slope(finish1(), 1)
    sm0()
    sb1()
    sg0(2)
    use_slope(slot(0, other), 0)
    use_slope(slot(-1, core), 0)
    use_slope(slot(1, core), 0)
    sf0()
    use_slope(slot(2, core), 0)
    sg0(5)
    use_slope(slot(-1, other), 0)
    sg0(6)
    use_slope(slot(1, other), 0)
    sg0(7, 8)
    use_slope(slot(2, other), 0)
    scatter(0, 1)
    sm1()
    use_slope(col, 1)
    sg1(2)
    use_slope(slot(0, other), 1)
    use_slope(slot(-1, core), 1)
    use_slope(slot(1, core), 1)
    sf1()
    use_slope(slot(2, core), 1)
    sg1(5)
    use_slope(slot(-1, other), 1)
    sg1(6)
    use_slope(slot(1, other), 1)
    sg1(7, 8)
    use_slope(slot(2, other), 1)
    scatter(1, 1)
    sc0()
    sc1()
    scatter(0, 2)

    back[...] = jnp.zeros_like(back)

    def back_step(i, _):
        def step(j, _):
            back[:, tile(j)] += (jnp.dot(slopes[0, i], pair(wout, i, 0, tile(j)), preferred_element_type=F32)
                                 + jnp.dot(slopes[1, i], pair(wout, i, 1, tile(j)), preferred_element_type=F32))
            return 0

        return lax.fori_loop(0, tiles, step, 0)

    lax.fori_loop(0, n_cols, back_step, 0)
    for c in gathers.values():
        c.wait_send()
    for path in range(2):
        for d in (1, -1):
            pl.semaphore_signal(credit, inc=1, device_id=toward(path, "f", d), device_id_type=MESH)
    scatter(1, 2)
    sh[...] = (back[...] * hid[...]).astype(BF16)

    def in_step(i, _):
        for u in range(2):
            turned[...] = latents[u, i].astype(F32).T.astype(BF16)

            def step(j, _):
                win[rows_of(i, u, half), tile(j)] = jnp.dot(
                    turned[...], sh[:, tile(j)], preferred_element_type=F32).astype(BF16)
                return 0

            lax.fori_loop(0, tiles, step, 0)
        return 0

    lax.fori_loop(0, n_cols, in_step, 0)
    pl.semaphore_wait(credit, 4)
    scatter(2, 1)
    scatter(0, 3)
    scatter(1, 3)
    scatter(2, 2)
    scatter(0, 4)
    scatter(1, 4)
    scatter(0, 5)
    scatter(1, 5)
    scatter(2, 3)
    scatter(2, 4)
    scatter(2, 5)


def hand_out(a, b, c, x, y, z, sem):
    copies = [pltpu.make_async_copy(s, d, sem.at[i]) for i, (s, d) in enumerate(((a, x), (b, y), (c, z)))]
    for c in copies:
        c.start()
    for c in copies:
        c.wait()


def per_device(noise, data, times, time_embed, norm_gain, w_in, w_out):
    n, width = noise.shape
    m = data.shape[0]
    wr, ffd = w_in.shape
    share = width // 8
    half = share // 2
    vm = pl.BlockSpec(memory_space=pltpu.VMEM)
    hbm = pl.BlockSpec(memory_space=pl.ANY)
    dma = pltpu.SemaphoreType.DMA
    outs = pl.pallas_call(
        kernel,
        out_shape=(
            jax.ShapeDtypeStruct((n, share), BF16),
            jax.ShapeDtypeStruct((wr, ffd), BF16),
            jax.ShapeDtypeStruct((ffd, wr), BF16),
        ),
        in_specs=[hbm, hbm, vm, vm, vm, hbm, vm],
        out_specs=(vm, vm, vm),
        scratch_shapes=[
            pltpu.VMEM((2, 8, n, half), BF16),
            pltpu.VMEM((width, ffd), BF16),
            pltpu.VMEM((width, ffd), BF16),
            pltpu.VMEM((width, ffd), BF16),
            pltpu.VMEM((width, ffd), BF16),
            pltpu.VMEM((2, 8, n, half), BF16),
            pltpu.VMEM((n, ffd), BF16),
            pltpu.VMEM((n, ffd), F32),
            pltpu.VMEM((n, ffd), F32),
            pltpu.VMEM((n, m), F32),
            pltpu.VMEM((n, m), BF16),
            pltpu.VMEM((n, share), F32),
            pltpu.VMEM((n, ffd), BF16),
            pltpu.VMEM((half, n), BF16),
            pltpu.VMEM((2, 4, n, half), BF16),
            pltpu.VMEM((2, 4, n, half), BF16),
            pltpu.VMEM((2, n, half), BF16),
            pltpu.VMEM((2, n, half), BF16),
            pltpu.VMEM((2, n, half), BF16),
            pltpu.VMEM((2, 2, n // 2, half), BF16),
            pltpu.VMEM((2, 2, n, half), BF16),
            pltpu.VMEM((2, n, half), F32),
            pltpu.VMEM((n, 128), F32),
            pltpu.VMEM((m, 128), F32),
            pltpu.VMEM((2, wr // 2, ffd), F32),
            pltpu.VMEM((ITERS, 2, m), F32),
            pltpu.VMEM((ITERS, 15, 2, m), F32),
            pltpu.VMEM((ITERS + 1, 2, n), F32),
            pltpu.VMEM((ITERS + 1, 7, 2, n), F32),
            dma((ITERS,)), dma((ITERS,)), dma((ITERS + 1,)), dma((ITERS + 1,)),
            dma((3, 2, 20)), dma((3, 2, 20)),
            dma((2, 2, 10)), dma((2, 2, 10)),
            dma((2, 2, 9)), dma((2, 2, 9)),
            dma((3, 2, 18)), dma((3, 2, 18)),
            dma((21,)),
            pltpu.SemaphoreType.REGULAR,
        ],
        compiler_params=pltpu.CompilerParams(
            collective_id=0, has_side_effects=True, vmem_limit_bytes=62 * 2**20
        ),
    )(noise, data, times, time_embed[None, :], norm_gain[None, :], w_in, w_out)
    return pl.pallas_call(
        hand_out,
        out_shape=tuple(jax.ShapeDtypeStruct(o.shape, o.dtype) for o in outs),
        in_specs=[hbm] * 3,
        out_specs=(hbm,) * 3,
        scratch_shapes=[dma((3,))],
    )(*outs)


def solution(mesh):
    in_specs = (
        P("rows", None),
        P("cols", None),
        P("rows"),
        P(),
        P(),
        P("rows", "cols"),
        P("cols", "rows"),
    )
    out_specs = (P("rows", "cols"), P("rows", "cols"), P("cols", "rows"))
    return jax.shard_map(
        per_device, mesh=mesh, in_specs=in_specs, out_specs=out_specs, check_vma=False
    )
```

```python
import functools
import math

import jax
import jax.numpy as jnp
from jax import lax
from jax.experimental import pallas as pl
from jax.experimental.pallas import tpu as pltpu
from jax.sharding import PartitionSpec as P

ITERS = 3
EPSILON = 0.01
MESH = pl.DeviceIdType.MESH
F32 = jnp.float32
BF16 = jnp.bfloat16
NT = (((1,), (1,)), ((), ()))
ORDER = (2, 1, 3, 0)


def ring(value):
    return lax.rem(value + 4, 4)


def tall(row, rows):
    return jnp.broadcast_to(row, (128, rows)).T[:, 0:1]


def flat(left, right):
    lane = lax.broadcasted_iota(jnp.int32, (left.shape[0], 128), 1)
    both = jnp.where(lane < 64, left, right).T
    return both[0:1], both[64:65]


def kernel(noise_hbm, data_hbm, times_ref, embed_ref, gain_ref, w_in_hbm, w_out_ref,
           target_ref, gin_ref, gout_ref,
           slopes, dbuf, win, wout, rx, latents, act, hid, back, a_ref, p_ref, state, sh,
           sibs, sibr, outs, rh, rf, own, nsq, dsq, final,
           csend, crecv, rsend, rrecv,
           cs, cr, rs, rr, ag_s, ag_r, xs, xr, ug_s, ug_r, gr_s, gr_r, loc, credit):
    n_rows, n_cols = 16, 8
    row = lax.axis_index("rows")
    col = lax.axis_index("cols")
    z, y = row // 4, lax.rem(row, 4)
    xx, core = col // 2, lax.rem(col, 2)
    n, width = noise_hbm.shape
    m = data_hbm.shape[0]
    share = width // n_cols
    wr, ffd = w_in_hbm.shape
    half = share // 2
    eighth = share // 4
    hn = n // 2
    tokens = n * n_rows

    def rdesc(src, dst, send, recv, to):
        return pltpu.make_async_remote_copy(src_ref=src, dst_ref=dst, send_sem=send, recv_sem=recv,
                                            device_id=to, device_id_type=MESH)

    def rcopy(*args):
        rdesc(*args).start()

    barrier = pltpu.get_barrier_semaphore()
    for d in range(1, n_rows):
        pl.semaphore_signal(barrier, inc=1, device_id=(lax.rem(row + d, n_rows), col), device_id_type=MESH)
    for d in range(1, n_cols):
        pl.semaphore_signal(barrier, inc=1, device_id=(row, lax.rem(col + d, n_cols)), device_id_type=MESH)

    def mine(i):
        return pl.ds(pl.multiple_of(i * wr, wr), wr)

    w_copy = pltpu.make_async_copy(w_in_hbm, win.at[mine(row)], loc.at[0])
    w_copy.start()

    def noise_copy(q):
        return pltpu.make_async_copy(noise_hbm.at[:, pl.ds(pl.multiple_of(q * half, half), half)],
                                     slopes.at[lax.rem(q, 2), q // 2], loc.at[5 + q])

    def data_copy(q):
        return pltpu.make_async_copy(data_hbm.at[:, pl.ds(pl.multiple_of(q * 2 * share, 2 * share), 2 * share)],
                                     dbuf.at[pl.ds(pl.multiple_of(q * m, m), m)], loc.at[1 + q])

    for q in range(4):
        for h in range(4):
            noise_copy(4 * q + h).start()
        data_copy(q).start()
    wout[mine(row)] = w_out_ref[...].astype(F32).T.astype(BF16)
    w_copy.wait()

    def place(path, f, s):
        return s * 4 + f if path == 0 else f * 4 + s

    def here(path):
        return (y, z) if path == 0 else (z, y)

    def piece(ref, unit, path, f, s, part=None):
        base, high = unit
        off = base + path * high + (high // 2 if part == 1 else 0)
        size = high if part is None else high // 2
        return ref.at[pl.ds(pl.multiple_of(place(path, ring(f), ring(s)) * wr + off, high // 2), size)]

    wide, low, up = (0, wr // 2), (0, wr // 4), (wr // 2, wr // 4)

    def toward(path, axis, d):
        f, s = here(path)
        if axis == "f":
            return (place(path, ring(f + d), s), col)
        return (place(path, f, ring(s + d)), col)

    routes = [
        ("f", 1, 0, 0, None), ("f", -1, 0, 0, None), ("s", 1, 0, 0, None), ("s", -1, 0, 0, None),
        ("f", 1, -1, 0, 0), ("f", -1, 1, 0, 1),
        ("s", 1, -1, 0, None), ("s", -1, -1, 0, None), ("s", 1, 1, 0, None), ("s", -1, 1, 0, None),
        ("s", 1, 0, -1, 0), ("s", -1, 0, 1, 1), ("s", 1, 2, 0, None), ("s", -1, 2, 0, None),
        ("s", 1, -1, -1, 0), ("s", -1, -1, 1, 1), ("s", 1, 1, -1, 0), ("s", -1, 1, 1, 1),
        ("s", 1, 2, -1, 0), ("s", -1, 2, 1, 1),
    ]

    def carry(w, path, i):
        axis, d, df, ds_, part = routes[i]
        f, s = here(path)
        spot = piece((win, wout, wout)[w], (wide, low, up)[w], path, f + df, s + ds_, part)
        return rdesc(spot, spot, ag_s.at[w, path, i], ag_r.at[w, path, i], toward(path, axis, d))

    sends = {"1": (0, 1, 2, 3), "2a": (4, 5, 6, 7, 8, 9), "2b": (10, 11), "3a": (12, 13), "3b": (14, 15),
             "3c": (16, 17), "4": (18, 19)}
    needs = {"2a": (0, 1), "2b": (2, 3), "3a": (4, 5), "3b": (6, 7), "3c": (8, 9), "4": (12, 13),
             "end": (10, 11, 14, 15, 16, 17, 18, 19)}

    def gather(w, *steps):
        for step in steps:
            for i in needs.get(step, ()):
                for path in range(2):
                    carry(w, path, i).wait_recv()
            for i in sends.get(step, ()):
                for path in range(2):
                    carry(w, path, i).start()

    plan = {
        "p0": [(0,"1"), (1,"1")],
        "c4": [(0,"2a","2b")],
        "k0r": [(2,"1")],
        "k1c": [(0,"3a")],
        "k1r": [(0,"3b")],
        "k2c": [(0,"3c"), (1,"2a")],
        "k2r": [(1,"2b"), (0,"4")],
        "t0": [(2,"2a")],
        "t2": [(2,"2b"), (1,"3a")],
        "t4": [(1,"3b")],
        "t5": [(1,"3c")],
        "h0": [(0,"end")],
        "h1": [(2,"3a"), (1,"4")],
        "h2": [(2,"3b"), (2,"3c")],
        "h4": [(2,"4")],
        "v0": [(1,"end")],
        "v1": [(2,"end")],
    }

    def at(point):
        for job in plan.get(point, ()):
            gather(*job)

    pl.semaphore_wait(barrier, n_rows + n_cols - 2)
    at("p0")

    def squares(value):
        value = value.astype(F32)
        value = value * value
        out = value[:, 0:128]
        for j in range(1, value.shape[1] // 128):
            out = out + value[:, j * 128 : (j + 1) * 128]
        return out

    a_ref[...] = jnp.zeros_like(a_ref)
    nsq[...] = jnp.zeros_like(nsq)
    dsq[...] = jnp.zeros_like(dsq)

    def cost_step(q, _):
        for h in range(4):
            noise_copy(4 * q + h).wait()
        data_copy(q).wait()
        total = None
        for h in range(4):
            term = lax.dot_general(slopes[h % 2, 2 * q + h // 2],
                                   dbuf[pl.ds(pl.multiple_of(q * m, m), m), h * half : (h + 1) * half], NT,
                                   preferred_element_type=F32)
            total = term if total is None else total + term
        a_ref[...] += total

        def noise_rows(i, _):
            at = pl.ds(pl.multiple_of(i * 32, 32), 32)
            value = squares(slopes[0, 2 * q, at, :])
            for h in range(1, 4):
                value = value + squares(slopes[h % 2, 2 * q + h // 2, at, :])
            nsq[at, :] += value
            return 0

        def data_rows(i, _):
            at = pl.ds(pl.multiple_of(i * 32, 32), 32)
            dsq[at, :] += squares(dbuf[pl.ds(pl.multiple_of(q * m + i * 32, 32), 32), :])
            return 0

        lax.fori_loop(0, n // 32, noise_rows, 0)
        lax.fori_loop(0, m // 32, data_rows, 0)
        return 0

    lax.fori_loop(0, 4, cost_step, 0)
    noise_sq = jnp.sum(nsq[...], axis=1, keepdims=True)
    data_sq = jnp.sum(dsq[...].T, axis=0, keepdims=True)
    a_ref[...] = (noise_sq + data_sq - 2.0 * a_ref[...]) * (1.0 / (width * EPSILON))
    base = -math.log(tokens)
    at("c4")

    def rows_swap(it):
        for d in range(1, n_rows):
            rcopy(csend.at[it], crecv.at[it, d - 1], cs.at[it], cr.at[it], (lax.rem(row + d, n_rows), col))

    def cols_swap(it):
        for d in range(1, n_cols):
            rcopy(rsend.at[it], rrecv.at[it, d - 1], rs.at[it], rr.at[it], (row, lax.rem(col + d, n_cols)))

    def await_all(ref, sem):
        pltpu.make_async_copy(ref, ref, sem).wait()

    def merge(got, top, tot):
        gt = got[:, 0, :]
        best = jnp.maximum(top, jnp.max(gt, axis=0, keepdims=True))
        total = tot * jnp.exp(top - best) + jnp.sum(got[:, 1, :] * jnp.exp(gt - best), axis=0, keepdims=True)
        return base - (best + jnp.log(total))

    def when(condition, *points):
        @pl.when(condition)
        def _():
            for point in points:
                at(point)

    def sweep(it, fg):
        x = fg[0] - a_ref[...]
        top = jnp.max(x, axis=0, keepdims=True)
        tot = jnp.sum(jnp.exp(x - top), axis=0, keepdims=True)
        csend[it, 0:1, :] = top
        csend[it, 1:2, :] = tot
        rows_swap(it)
        for i in range(ITERS):
            when(it == i, ("k0c", "k1c", "k2c")[i])
        await_all(crecv.at[it], cr.at[it])
        g = merge(crecv[it], top, tot)

        x = g - a_ref[...]
        top = jnp.max(x, axis=1, keepdims=True)
        tot = jnp.sum(jnp.exp(x - top), axis=1, keepdims=True)
        top, tot = flat(top, tot)
        rsend[it, 0:1, :] = top
        rsend[it, 1:2, :] = tot
        cols_swap(it)
        for i in range(ITERS):
            when(it == i, ("k0r", "k1r", "k2r")[i])
        await_all(rrecv.at[it], rr.at[it])
        return tall(merge(rrecv[it], top, tot), n), g

    f, g = lax.fori_loop(0, ITERS, sweep, (jnp.zeros((n, 1), F32), jnp.zeros((1, m), F32)))
    p_ref[...] = (float(tokens) * jnp.exp(f + g - a_ref[...])).astype(BF16)
    for it in range(ITERS):
        await_all(crecv.at[it], cs.at[it])
        await_all(rrecv.at[it], rs.at[it])

    def at_x(d, k):
        return (row, ring(xx + d) * 2 + k)

    def reduce_copy(t, u, i):
        lo, hi = pl.ds(0, hn), pl.ds(hn, hn)
        if not isinstance(i, int):
            src, dst, to = sibs.at[u, i], sibr.at[u, i], at_x(0, 1 - core)
        else:
            src, dst, d = {
                4: (outs.at[u, 0, lo], rh.at[u, 0], 1),
                5: (outs.at[u, 0, hi], rh.at[u, 1], -1),
                6: (outs.at[u, 1, hi], rf.at[u, 0, hi], 1),
                7: (outs.at[u, 2, lo], rf.at[u, 1, lo], -1),
                8: (outs.at[u, 1, lo], rf.at[u, 0, lo], 1),
                9: (outs.at[u, 2, hi], rf.at[u, 1, hi], -1),
            }[i]
            to = at_x(d, core)
        return rdesc(src, dst, xs.at[t, u, i], xr.at[t, u, i], to)

    def cols_reduce(make, t, u):
        def block_step(i, _):
            d = jnp.where(i == 0, 2, jnp.where(i == 3, 0, 2 * i - 1))
            sibs[u, i] = make(ring(xx + d) * 2 + 1 - core, u).astype(BF16)
            reduce_copy(t, u, i).start()
            value = make(ring(xx + d) * 2 + core, u)
            reduce_copy(t, u, i).wait_recv()
            value = value + sibr[u, i].astype(F32)
            own[u] = value
            outs[u, i] = value.astype(BF16)

            @pl.when(i == 0)
            def _():
                reduce_copy(t, u, 4).start()
                reduce_copy(t, u, 5).start()

            @pl.when(i == 1)
            def _():
                reduce_copy(t, u, 6).start()

            @pl.when(i == 2)
            def _():
                reduce_copy(t, u, 7).start()

            return 0

        lax.fori_loop(0, 4, block_step, 0)
        reduce_copy(t, u, 4).wait_recv()
        outs[u, 1, 0:hn] = (outs[u, 1, 0:hn].astype(F32) + rh[u, 0].astype(F32)).astype(BF16)
        reduce_copy(t, u, 8).start()
        reduce_copy(t, u, 5).wait_recv()
        outs[u, 2, hn:n] = (outs[u, 2, hn:n].astype(F32) + rh[u, 1].astype(F32)).astype(BF16)
        reduce_copy(t, u, 9).start()

    def reduced(t, u):
        for i in (6, 7, 8, 9):
            reduce_copy(t, u, i).wait_recv()
        value = own[u] + rf[u, 0].astype(F32) + rf[u, 1].astype(F32)
        for i in range(4):
            reduce_copy(t, u, jnp.int32(i)).wait_send()
        for i in range(4, 10):
            reduce_copy(t, u, i).wait_send()
        return value

    def slot(d, k):
        return ring(xx + d) * 2 + k

    other = 1 - core

    def visit(j):
        d = jnp.where(j < 2, 0, jnp.where(j >= 6, 2, 2 * lax.rem(j, 2) - 1))
        k = jnp.where((j == 1) | (j == 4) | (j == 5) | (j == 7), other, core)
        return slot(d, k)

    def spread(ref, t, u):
        def copy(i):
            lo, hi = pl.ds(0, hn), pl.ds(hn, hn)
            twin = at_x(0, other)
            src, to = {
                0: (ref.at[u, col], at_x(1, core)),
                1: (ref.at[u, col], at_x(-1, core)),
                2: (ref.at[u, col], twin),
                3: (ref.at[u, slot(-1, core), lo], at_x(1, core)),
                4: (ref.at[u, slot(1, core), hi], at_x(-1, core)),
                5: (ref.at[u, slot(-1, core)], twin),
                6: (ref.at[u, slot(1, core)], twin),
                7: (ref.at[u, slot(2, core), lo], twin),
                8: (ref.at[u, slot(2, core), hi], twin),
            }[i]
            return rdesc(src, src, ug_s.at[t, u, i], ug_r.at[t, u, i], to)

        def begin():
            for i in range(3):
                copy(i).start()

        def middle():
            copy(0).wait_recv()
            copy(3).start()
            copy(5).start()
            copy(1).wait_recv()
            copy(4).start()
            copy(6).start()

        def finish():
            copy(3).wait_recv()
            copy(7).start()
            copy(4).wait_recv()
            copy(8).start()

        def got(*which):
            for i in which:
                copy(i).wait_recv()

        def close():
            for i in range(9):
                copy(i).wait_send()

        return begin, middle, finish, got, close

    tiles = ffd // 256

    def tile(j):
        return pl.ds(pl.multiple_of(j * 256, 256), 256)

    def rows_of(i, u, size):
        return pl.ds(pl.multiple_of(i * share + u * size, size), size)

    def target_block(fb, u):
        rows_at = pl.ds(pl.multiple_of(fb // 2 * m, m), m)
        lanes = pl.ds(pl.multiple_of(lax.rem(fb, 2) * share + u * half, half), half)
        return jnp.dot(p_ref[...], dbuf[rows_at, lanes], preferred_element_type=F32)

    t = tall(times_ref[...][None, :], n)

    def make_state(value, u):
        target = value.astype(BF16)
        target_ref[:, u * half : (u + 1) * half] = target
        target = target.astype(F32)
        noise = slopes[u, col].astype(F32)
        lanes = pl.ds(pl.multiple_of(col * share + u * half, half), half)
        st = (1.0 - t) * noise + t * target + t * embed_ref[:, lanes]
        latents[u, col] = (st * gain_ref[:, lanes]).astype(BF16)
        state[:, u * half : (u + 1) * half] = st - (target - noise)
        return jnp.sum(st * st, axis=1, keepdims=True)

    hb0, hm0, hf0, hg0, hc0 = spread(latents, 0, 0)
    hb1, hm1, hf1, hg1, hc1 = spread(latents, 0, 1)

    def target_half(u, _):
        when(u == 0, "t0")
        when(u == 1, "t2")
        cols_reduce(target_block, 0, u)
        return 0

    lax.fori_loop(0, 2, target_half, 0)
    at("t4")
    part = make_state(reduced(0, 0), 0)
    hb0()
    at("t5")
    part = part + make_state(reduced(0, 1), 1)
    part, _ = flat(part, part)
    rsend[ITERS, 0:1, :] = part
    rsend[ITERS, 1:2, :] = part
    cols_swap(ITERS)
    hm0()
    hb1()
    at("h0")
    hid[...] = jnp.zeros_like(hid)

    def hidden_step(j, _):
        @pl.when(j == 1)
        def _():
            at("h1")
            hf0()
            hm1()
            at("h2")
            hg0(2)
            hg1(2)

        @pl.when(j == 3)
        def _():
            hf1()

        @pl.when(j == 4)
        def _():
            at("h3")
            hg0(5)
            hg1(5)

        @pl.when(j == 5)
        def _():
            hg0(6)
            hg1(6)

        @pl.when(j == 7)
        def _():
            at("h4")
            hg0(7, 8)
            hg1(7, 8)

        i = visit(j)
        hid[...] += (jnp.dot(latents[0, i], win[rows_of(i, 0, half), :], preferred_element_type=F32)
                     + jnp.dot(latents[1, i], win[rows_of(i, 1, half), :], preferred_element_type=F32))
        return 0

    lax.fori_loop(0, n_cols, hidden_step, 0)
    hc0()
    hc1()
    await_all(rrecv.at[ITERS], rr.at[ITERS])
    await_all(rrecv.at[ITERS], rs.at[ITERS])
    square = part + jnp.sum(rrecv[ITERS][:, 0, :], axis=0, keepdims=True)
    scale = tall(lax.rsqrt(square / width + 1e-6), n)

    def gelu_step(j, _):
        h = hid[:, tile(j)] * scale
        c = math.sqrt(2.0 / math.pi)
        h2 = h * h
        th = jnp.tanh(c * (h + 0.044715 * (h2 * h)))
        act[:, tile(j)] = (0.5 * h * (1.0 + th)).astype(BF16)
        slope_of = 0.5 * (1.0 + th) + 0.5 * h * (1.0 - th * th) * (c * (1.0 + (3 * 0.044715) * h2))
        hid[:, tile(j)] = slope_of * scale
        return 0

    lax.fori_loop(0, tiles, gelu_step, 0)
    at("v0")

    def pair(ref, i, u, at):
        lo = ref[pl.ds(pl.multiple_of(i * share + u * eighth, eighth), eighth), at]
        hi = ref[pl.ds(pl.multiple_of(i * share + half + u * eighth, eighth), eighth), at]
        return jnp.concatenate([lo, hi], axis=0)

    def velocity_block(fb, u):
        return lax.dot_general(act[...], pair(wout, fb, u, slice(None)), NT, preferred_element_type=F32)

    def make_slope(value, u):
        lo = state[:, u * eighth : (u + 1) * eighth]
        hi = state[:, half + u * eighth : half + (u + 1) * eighth]
        slopes[u, col] = ((jnp.concatenate([lo, hi], axis=1) + value) * (1.0 / math.sqrt(tokens))).astype(BF16)

    TN = (((0,), (0,)), ((), ()))

    def use_slope(i, u):
        value = lax.dot_general(slopes[u, i], act[...], TN, preferred_element_type=F32).astype(BF16)
        dbuf[pl.ds(pl.multiple_of(i * share + u * eighth, eighth), eighth), :] = value[:eighth]
        dbuf[pl.ds(pl.multiple_of(i * share + half + u * eighth, eighth), eighth), :] = value[eighth:]

    def rx_at(ref, base, unit, path, j, part=None):
        high = unit[1]
        off = high // 2 if part == 1 else 0
        size = high if part is None else high // 2
        return ref.at[pl.ds(base + (path * 16 + j) * high + off, size)]

    def shift(w, path, i):
        ref = (dbuf, dbuf, win)[w]
        unit = (low, up, wide)[w]
        f, s = here(path)
        if i < 4:
            e, axis, d = (2, 1, 3, 0)[i], "f", 1 if i < 2 else -1
            src, dst = (f + 2, s + e, None), (i, None)
        elif i < 12:
            e, axis, d = i % 4, "f", 1 if i < 8 else -1
            src, dst = (f + d, s + e, None), (i, None)
        else:
            axis, d = "s", 1 if i % 2 == 0 else -1
            src, dst = {
                12: ((f, s + 2, 0), (12, 0)), 13: ((f, s + 2, 1), (12, 1)),
                14: ((f, s + 1, 1), (13, 1)), 15: ((f, s - 1, 0), (14, 0)),
                16: ((f, s + 1, 0), (13, 0)), 17: ((f, s - 1, 1), (14, 1)),
            }[i]
        return rdesc(piece(ref, unit, path, *src), landing(w, path, *dst),
                     gr_s.at[w, path, i], gr_r.at[w, path, i], toward(path, axis, d))

    def landing(w, path, j, part=None):
        return rx_at((rx, rx, wout)[w], (0, width // 2, 0)[w], (low, up, wide)[w], path, j, part)

    def add(at, *more):
        def rows_step(r, _):
            rows = pl.ds(pl.multiple_of(r * 32, 32), 32)
            value = at[rows, :].astype(F32)
            for one in more:
                value = value + one[rows, :].astype(F32)
            at[rows, :] = value.astype(BF16)
            return 0

        lax.fori_loop(0, at.shape[0] // 32, rows_step, 0)

    def scatter(w, step):
        ref = (dbuf, dbuf, win)[w]
        unit = (low, up, wide)[w]
        high = unit[1]
        if step == 1:
            for i in (0, 1, 2, 3, 4, 7, 9, 10):
                for path in range(2):
                    shift(w, path, i).start()
        for path in range(2):
            f, s = here(path)
            if step == 2:
                for j in range(2):
                    for d, i, e in ((1, j, (2, 1)[j]), (-1, 2 + j, (3, 0)[j])):
                        shift(w, path, i).wait_recv()
                        add(piece(ref, unit, path, f + d, s + e), landing(w, path, i))
                        shift(w, path, (4 if d == 1 else 8) + e).start()
            if step == 3:
                for e in ORDER:
                    shift(w, path, 4 + e).wait_recv()
                    shift(w, path, 8 + e).wait_recv()
                    add(piece(ref, unit, path, f, s + e), landing(w, path, 4 + e), landing(w, path, 8 + e))
                    for i in {2: (12, 13), 1: (14,), 3: (15,), 0: ()}[e]:
                        shift(w, path, i).start()
            if step == 4:
                shift(w, path, 12).wait_recv()
                add(piece(ref, unit, path, f, s + 1, 0), landing(w, path, 12, 0))
                shift(w, path, 16).start()
                shift(w, path, 13).wait_recv()
                add(piece(ref, unit, path, f, s - 1, 1), landing(w, path, 12, 1))
                shift(w, path, 17).start()
            if step == 5:
                for i in range(14, 18):
                    shift(w, path, i).wait_recv()
                value = (piece(ref, unit, path, f, s)[...].astype(F32) + landing(w, path, 13)[...].astype(F32)
                         + landing(w, path, 14)[...].astype(F32))
                if w < 2:
                    final[w, path * high : (path + 1) * high, :] = value
                    if path == 1:
                        gout_ref[:, w * 2 * high : (w + 1) * 2 * high] = final[w].T.astype(BF16)
                else:
                    gin_ref[path * high : (path + 1) * high, :] = value.astype(BF16)
                for i in range(18):
                    shift(w, path, i).wait_send()

    sb0, sm0, sf0, sg0, sc0 = spread(slopes, 1, 0)
    sb1, sm1, sf1, sg1, sc1 = spread(slopes, 1, 1)

    def velocity_half(u, _):
        when(u == 1, "v1")
        cols_reduce(velocity_block, 1, u)
        return 0

    lax.fori_loop(0, 2, velocity_half, 0)
    make_slope(reduced(1, 0), 0)
    sb0()

    def slope_step(jj, _):
        def on(number, *calls):
            @pl.when(jj == number)
            def _():
                for call in calls:
                    call()

        on(1, lambda: make_slope(reduced(1, 1), 1), sm0, sb1, lambda: sg0(2))
        on(4, sf0, lambda: sg0(5))
        on(5, lambda: sg0(6))
        on(7, lambda: sg0(7, 8))
        on(8, lambda: scatter(0, 1), sm1)
        on(9, lambda: sg1(2))
        on(12, sf1, lambda: sg1(5))
        on(13, lambda: sg1(6))
        on(15, lambda: sg1(7, 8))
        use_slope(visit(lax.rem(jj, 8)), jj // 8)
        return 0

    lax.fori_loop(0, 16, slope_step, 0)
    scatter(1, 1)
    sc0()
    sc1()
    scatter(0, 2)

    every = slice(None)
    back[...] = jnp.zeros_like(back)

    def back_step(i, _):
        back[...] += (jnp.dot(slopes[0, i], pair(wout, i, 0, every), preferred_element_type=F32)
                      + jnp.dot(slopes[1, i], pair(wout, i, 1, every), preferred_element_type=F32))
        return 0

    lax.fori_loop(0, n_cols, back_step, 0)
    for w in range(3):
        for path in range(2):
            for i in range(20):
                carry(w, path, i).wait_send()
    for path in range(2):
        for d in (1, -1):
            pl.semaphore_signal(credit, inc=1, device_id=toward(path, "f", d), device_id_type=MESH)
    scatter(1, 2)
    sh[...] = (back[...] * hid[...]).astype(BF16)

    def in_step(i, _):
        win[pl.ds(pl.multiple_of(i * half, half), half), :] = lax.dot_general(
            latents[lax.rem(i, 2), i // 2], sh[...], TN, preferred_element_type=F32).astype(BF16)
        return 0

    lax.fori_loop(0, 2 * n_cols, in_step, 0)
    pl.semaphore_wait(credit, 4)
    scatter(2, 1)
    scatter(0, 3)
    scatter(1, 3)
    scatter(2, 2)
    scatter(0, 4)
    scatter(1, 4)
    scatter(0, 5)
    scatter(1, 5)
    scatter(2, 3)
    scatter(2, 4)
    scatter(2, 5)


def hand_out(a, b, c, x, y, z, *rest):
    sem = rest[3]
    ins = [pltpu.make_async_copy(s, v, sem.at[i]) for i, (s, v) in enumerate(zip((a, b, c), rest))]
    outs = [pltpu.make_async_copy(v, d, sem.at[3 + i]) for i, (v, d) in enumerate(zip(rest, (x, y, z)))]
    for c in ins:
        c.start()
    for i in range(3):
        ins[i].wait()
        outs[i].start()
    for c in outs:
        c.wait()


def per_device(noise, data, times, time_embed, norm_gain, w_in, w_out):
    n, width = noise.shape
    m = data.shape[0]
    wr, ffd = w_in.shape
    share = width // 8
    half = share // 2
    vm = pl.BlockSpec(memory_space=pltpu.VMEM)
    hbm = pl.BlockSpec(memory_space=pl.ANY)
    dma = pltpu.SemaphoreType.DMA
    outs = pl.pallas_call(
        kernel,
        out_shape=(
            jax.ShapeDtypeStruct((n, share), BF16),
            jax.ShapeDtypeStruct((wr, ffd), BF16),
            jax.ShapeDtypeStruct((ffd, wr), BF16),
        ),
        in_specs=[hbm, hbm, vm, vm, vm, hbm, vm],
        out_specs=(vm, vm, vm),
        scratch_shapes=[
            pltpu.VMEM((2, 8, n, half), BF16),
            pltpu.VMEM((width, ffd), BF16),
            pltpu.VMEM((width, ffd), BF16),
            pltpu.VMEM((width, ffd), BF16),
            pltpu.VMEM((width, ffd), BF16),
            pltpu.VMEM((2, 8, n, half), BF16),
            pltpu.VMEM((n, ffd), BF16),
            pltpu.VMEM((n, ffd), F32),
            pltpu.VMEM((n, ffd), F32),
            pltpu.VMEM((n, m), F32),
            pltpu.VMEM((n, m), BF16),
            pltpu.VMEM((n, share), F32),
            pltpu.VMEM((n, ffd), BF16),
            pltpu.VMEM((2, 4, n, half), BF16),
            pltpu.VMEM((2, 4, n, half), BF16),
            pltpu.VMEM((2, 4, n, half), BF16),
            pltpu.VMEM((2, 2, n // 2, half), BF16),
            pltpu.VMEM((2, 2, n, half), BF16),
            pltpu.VMEM((2, n, half), F32),
            pltpu.VMEM((n, 128), F32),
            pltpu.VMEM((m, 128), F32),
            pltpu.VMEM((2, wr // 2, ffd), F32),
            pltpu.VMEM((ITERS, 2, m), F32),
            pltpu.VMEM((ITERS, 15, 2, m), F32),
            pltpu.VMEM((ITERS + 1, 2, n), F32),
            pltpu.VMEM((ITERS + 1, 7, 2, n), F32),
            dma((ITERS,)), dma((ITERS,)), dma((ITERS + 1,)), dma((ITERS + 1,)),
            dma((3, 2, 20)), dma((3, 2, 20)),
            dma((2, 2, 10)), dma((2, 2, 10)),
            dma((2, 2, 9)), dma((2, 2, 9)),
            dma((3, 2, 18)), dma((3, 2, 18)),
            dma((21,)),
            pltpu.SemaphoreType.REGULAR,
        ],
        compiler_params=pltpu.CompilerParams(
            collective_id=0, has_side_effects=True, vmem_limit_bytes=62 * 2**20
        ),
    )(noise, data, times, time_embed[None, :], norm_gain[None, :], w_in, w_out)
    return pl.pallas_call(
        hand_out,
        out_shape=tuple(jax.ShapeDtypeStruct(o.shape, o.dtype) for o in outs),
        in_specs=[hbm] * 3,
        out_specs=(hbm,) * 3,
        scratch_shapes=[pltpu.VMEM(o.shape, o.dtype) for o in outs] + [dma((6,))],
    )(*outs)


def solution(mesh):
    in_specs = (
        P("rows", None),
        P("cols", None),
        P("rows"),
        P(),
        P(),
        P("rows", "cols"),
        P("cols", "rows"),
    )
    out_specs = (P("rows", "cols"), P("rows", "cols"), P("cols", "rows"))
    return jax.shard_map(
        per_device, mesh=mesh, in_specs=in_specs, out_specs=out_specs, check_vma=False
    )
```

```python
import functools
import math

import jax
import jax.numpy as jnp
from jax import lax
from jax.experimental import pallas as pl
from jax.experimental.pallas import tpu as pltpu
from jax.sharding import PartitionSpec as P

ITERS = 3
EPSILON = 0.01
MESH = pl.DeviceIdType.MESH
F32 = jnp.float32
BF16 = jnp.bfloat16
NT = (((1,), (1,)), ((), ()))
ORDER = (2, 1, 3, 0)


def ring(value):
    return lax.rem(value + 4, 4)


def tall(row, rows):
    return jnp.broadcast_to(row, (128, rows)).T[:, 0:1]


def flat(left, right):
    lane = lax.broadcasted_iota(jnp.int32, (left.shape[0], 128), 1)
    both = jnp.where(lane < 64, left, right).T
    return both[0:1], both[64:65]


def kernel(noise_hbm, data_hbm, times_ref, embed_ref, gain_ref, w_in_hbm, w_out_ref,
           target_ref, gin_ref, gout_ref,
           slopes, dbuf, win, wout, rx, latents, act, hid, back, a_ref, p_ref, state, sh,
           sibs, sibr, outs, rh, rf, own, nsq, dsq, final,
           csend, crecv, rsend, rrecv,
           cs, cr, rs, rr, ag_s, ag_r, xs, xr, ug_s, ug_r, gr_s, gr_r, loc, credit):
    n_rows, n_cols = 16, 8
    row = lax.axis_index("rows")
    col = lax.axis_index("cols")
    z, y = row // 4, lax.rem(row, 4)
    xx, core = col // 2, lax.rem(col, 2)
    n, width = noise_hbm.shape
    m = data_hbm.shape[0]
    share = width // n_cols
    wr, ffd = w_in_hbm.shape
    half = share // 2
    eighth = share // 4
    hn = n // 2
    tokens = n * n_rows

    def rdesc(src, dst, send, recv, to):
        return pltpu.make_async_remote_copy(src_ref=src, dst_ref=dst, send_sem=send, recv_sem=recv,
                                            device_id=to, device_id_type=MESH)

    def rcopy(*args):
        rdesc(*args).start()

    barrier = pltpu.get_barrier_semaphore()
    for d in range(1, n_rows):
        pl.semaphore_signal(barrier, inc=1, device_id=(lax.rem(row + d, n_rows), col), device_id_type=MESH)
    for d in range(1, n_cols):
        pl.semaphore_signal(barrier, inc=1, device_id=(row, lax.rem(col + d, n_cols)), device_id_type=MESH)

    def mine(i):
        return pl.ds(pl.multiple_of(i * wr, wr), wr)

    w_copy = pltpu.make_async_copy(w_in_hbm, win.at[mine(row)], loc.at[0])
    w_copy.start()

    def noise_copy(q):
        return pltpu.make_async_copy(noise_hbm.at[:, pl.ds(pl.multiple_of(q * half, half), half)],
                                     slopes.at[lax.rem(q, 2), q // 2], loc.at[5 + q])

    def data_copy(q):
        return pltpu.make_async_copy(data_hbm.at[:, pl.ds(pl.multiple_of(q * 2 * share, 2 * share), 2 * share)],
                                     dbuf.at[pl.ds(pl.multiple_of(q * m, m), m)], loc.at[1 + q])

    for q in range(4):
        for h in range(4):
            noise_copy(4 * q + h).start()
        data_copy(q).start()
    wout[mine(row)] = w_out_ref[...].astype(F32).T.astype(BF16)
    w_copy.wait()

    def place(path, f, s):
        return s * 4 + f if path == 0 else f * 4 + s

    def here(path):
        return (y, z) if path == 0 else (z, y)

    def piece(ref, unit, path, f, s, part=None):
        base, high = unit
        off = base + path * high + (high // 2 if part == 1 else 0)
        size = high if part is None else high // 2
        return ref.at[pl.ds(pl.multiple_of(place(path, ring(f), ring(s)) * wr + off, high // 2), size)]

    wide, low, up = (0, wr // 2), (0, wr // 4), (wr // 2, wr // 4)

    def toward(path, axis, d):
        f, s = here(path)
        if axis == "f":
            return (place(path, ring(f + d), s), col)
        return (place(path, f, ring(s + d)), col)

    routes = [
        ("f", 1, 0, 0, None), ("f", -1, 0, 0, None), ("s", 1, 0, 0, None), ("s", -1, 0, 0, None),
        ("f", 1, -1, 0, 0), ("f", -1, 1, 0, 1),
        ("s", 1, -1, 0, None), ("s", -1, -1, 0, None), ("s", 1, 1, 0, None), ("s", -1, 1, 0, None),
        ("s", 1, 0, -1, 0), ("s", -1, 0, 1, 1), ("s", 1, 2, 0, None), ("s", -1, 2, 0, None),
        ("s", 1, -1, -1, 0), ("s", -1, -1, 1, 1), ("s", 1, 1, -1, 0), ("s", -1, 1, 1, 1),
        ("s", 1, 2, -1, 0), ("s", -1, 2, 1, 1),
    ]

    def carry(w, path, i):
        axis, d, df, ds_, part = routes[i]
        f, s = here(path)
        spot = piece((win, wout, wout)[w], (wide, low, up)[w], path, f + df, s + ds_, part)
        return rdesc(spot, spot, ag_s.at[w, path, i], ag_r.at[w, path, i], toward(path, axis, d))

    sends = {"1": (0, 1, 2, 3), "2a": (4, 5, 6, 7, 8, 9), "2b": (10, 11), "3a": (12, 13), "3b": (14, 15),
             "3c": (16, 17), "4": (18, 19), "2x": (4, 5, 6, 7), "2y": (8, 9, 10, 11), "3x": (12, 13, 14, 15)}
    needs = {"2x": (0, 1), "2y": (2, 3), "3x": (4, 5, 6, 7), "2a": (0, 1), "2b": (2, 3), "3a": (4, 5), "3b": (6, 7), "3c": (8, 9), "4": (12, 13),
             "end": (10, 11, 14, 15, 16, 17, 18, 19)}

    def gather(w, *steps):
        for step in steps:
            for i in needs.get(step, ()):
                for path in range(2):
                    carry(w, path, i).wait_recv()
            for i in sends.get(step, ()):
                for path in range(2):
                    carry(w, path, i).start()

    plan = {
        "p0": [(0,"1"), (1,"1")],
        "k0c": [(0,"2x")],
        "k1c": [(0,"2y")],
        "k2c": [(0,"3x")],
        "t0": [(0,"3c"), (2,"1")],
        "t2": [(0,"4"), (1,"2a","2b")],
        "t4": [(2,"2x")],
        "h0": [(0,"end"), (1,"3a","3b","3c"), (2,"2y")],
        "h2": [(1,"4")],
        "h3": [(2,"3x")],
        "h4": [(2,"3c")],
        "v0": [(2,"4"), (1,"end")],
        "v1": [(2,"end")],
    }

    def at(point):
        for job in plan.get(point, ()):
            gather(*job)

    pl.semaphore_wait(barrier, n_rows + n_cols - 2)
    at("p0")

    def squares(value):
        value = value.astype(F32)
        value = value * value
        out = value[:, 0:128]
        for j in range(1, value.shape[1] // 128):
            out = out + value[:, j * 128 : (j + 1) * 128]
        return out

    a_ref[...] = jnp.zeros_like(a_ref)
    nsq[...] = jnp.zeros_like(nsq)
    dsq[...] = jnp.zeros_like(dsq)

    def cost_step(q, _):
        for h in range(4):
            noise_copy(4 * q + h).wait()
        data_copy(q).wait()
        total = None
        for h in range(4):
            term = lax.dot_general(slopes[h % 2, 2 * q + h // 2],
                                   dbuf[pl.ds(pl.multiple_of(q * m, m), m), h * half : (h + 1) * half], NT,
                                   preferred_element_type=F32)
            total = term if total is None else total + term
        a_ref[...] += total

        def noise_rows(i, _):
            at = pl.ds(pl.multiple_of(i * 32, 32), 32)
            value = squares(slopes[0, 2 * q, at, :])
            for h in range(1, 4):
                value = value + squares(slopes[h % 2, 2 * q + h // 2, at, :])
            nsq[at, :] += value
            return 0

        def data_rows(i, _):
            at = pl.ds(pl.multiple_of(i * 32, 32), 32)
            dsq[at, :] += squares(dbuf[pl.ds(pl.multiple_of(q * m + i * 32, 32), 32), :])
            return 0

        lax.fori_loop(0, n // 32, noise_rows, 0)
        lax.fori_loop(0, m // 32, data_rows, 0)
        return 0

    lax.fori_loop(0, 4, cost_step, 0)
    noise_sq = jnp.sum(nsq[...], axis=1, keepdims=True)
    data_sq = jnp.sum(dsq[...].T, axis=0, keepdims=True)
    a_ref[...] = (noise_sq + data_sq - 2.0 * a_ref[...]) * (1.0 / (width * EPSILON))
    base = -math.log(tokens)
    at("c4")

    def rows_swap(it):
        for d in range(1, n_rows):
            rcopy(csend.at[it], crecv.at[it, d - 1], cs.at[it], cr.at[it], (lax.rem(row + d, n_rows), col))

    def cols_swap(it):
        for d in range(1, n_cols):
            rcopy(rsend.at[it], rrecv.at[it, d - 1], rs.at[it], rr.at[it], (row, lax.rem(col + d, n_cols)))

    def await_all(ref, sem):
        pltpu.make_async_copy(ref, ref, sem).wait()

    def merge(got, top, tot):
        gt = got[:, 0, :]
        best = jnp.maximum(top, jnp.max(gt, axis=0, keepdims=True))
        total = tot * jnp.exp(top - best) + jnp.sum(got[:, 1, :] * jnp.exp(gt - best), axis=0, keepdims=True)
        return base - (best + jnp.log(total))

    def when(condition, *points):
        @pl.when(condition)
        def _():
            for point in points:
                at(point)

    def sweep(it, fg):
        x = fg[0] - a_ref[...]
        top = jnp.max(x, axis=0, keepdims=True)
        tot = jnp.sum(jnp.exp(x - top), axis=0, keepdims=True)
        csend[it, 0:1, :] = top
        csend[it, 1:2, :] = tot
        rows_swap(it)
        for i in range(ITERS):
            when(it == i, ("k0c", "k1c", "k2c")[i])
        await_all(crecv.at[it], cr.at[it])
        g = merge(crecv[it], top, tot)

        x = g - a_ref[...]
        top = jnp.max(x, axis=1, keepdims=True)
        tot = jnp.sum(jnp.exp(x - top), axis=1, keepdims=True)
        top, tot = flat(top, tot)
        rsend[it, 0:1, :] = top
        rsend[it, 1:2, :] = tot
        cols_swap(it)
        for i in range(ITERS):
            when(it == i, ("k0r", "k1r", "k2r")[i])
        await_all(rrecv.at[it], rr.at[it])
        return tall(merge(rrecv[it], top, tot), n), g

    f, g = lax.fori_loop(0, ITERS, sweep, (jnp.zeros((n, 1), F32), jnp.zeros((1, m), F32)))
    p_ref[...] = (float(tokens) * jnp.exp(f + g - a_ref[...])).astype(BF16)
    for it in range(ITERS):
        await_all(crecv.at[it], cs.at[it])
        await_all(rrecv.at[it], rs.at[it])

    def at_x(d, k):
        return (row, ring(xx + d) * 2 + k)

    def reduce_copy(t, u, i):
        lo, hi = pl.ds(0, hn), pl.ds(hn, hn)
        if not isinstance(i, int):
            src, dst, to = sibs.at[u, i], sibr.at[u, i], at_x(0, 1 - core)
        else:
            src, dst, d = {
                4: (outs.at[u, 0, lo], rh.at[u, 0], 1),
                5: (outs.at[u, 0, hi], rh.at[u, 1], -1),
                6: (outs.at[u, 1, hi], rf.at[u, 0, hi], 1),
                7: (outs.at[u, 2, lo], rf.at[u, 1, lo], -1),
                8: (outs.at[u, 1, lo], rf.at[u, 0, lo], 1),
                9: (outs.at[u, 2, hi], rf.at[u, 1, hi], -1),
            }[i]
            to = at_x(d, core)
        return rdesc(src, dst, xs.at[t, u, i], xr.at[t, u, i], to)

    def cols_reduce(make, t, u):
        def block_step(i, _):
            d = jnp.where(i == 0, 2, jnp.where(i == 3, 0, 2 * i - 1))
            sibs[u, i] = make(ring(xx + d) * 2 + 1 - core, u).astype(BF16)
            reduce_copy(t, u, i).start()
            value = make(ring(xx + d) * 2 + core, u)
            reduce_copy(t, u, i).wait_recv()
            value = value + sibr[u, i].astype(F32)
            own[u] = value
            outs[u, i] = value.astype(BF16)

            @pl.when(i == 0)
            def _():
                reduce_copy(t, u, 4).start()
                reduce_copy(t, u, 5).start()

            @pl.when(i == 1)
            def _():
                reduce_copy(t, u, 6).start()

            @pl.when(i == 2)
            def _():
                reduce_copy(t, u, 7).start()

            return 0

        lax.fori_loop(0, 4, block_step, 0)
        reduce_copy(t, u, 4).wait_recv()
        outs[u, 1, 0:hn] = (outs[u, 1, 0:hn].astype(F32) + rh[u, 0].astype(F32)).astype(BF16)
        reduce_copy(t, u, 8).start()
        reduce_copy(t, u, 5).wait_recv()
        outs[u, 2, hn:n] = (outs[u, 2, hn:n].astype(F32) + rh[u, 1].astype(F32)).astype(BF16)
        reduce_copy(t, u, 9).start()

    def reduced(t, u):
        for i in (6, 7, 8, 9):
            reduce_copy(t, u, i).wait_recv()
        value = own[u] + rf[u, 0].astype(F32) + rf[u, 1].astype(F32)
        for i in range(4):
            reduce_copy(t, u, jnp.int32(i)).wait_send()
        for i in range(4, 10):
            reduce_copy(t, u, i).wait_send()
        return value

    def slot(d, k):
        return ring(xx + d) * 2 + k

    other = 1 - core

    def visit(j):
        d = jnp.where(j < 2, 0, jnp.where(j >= 6, 2, 2 * lax.rem(j, 2) - 1))
        k = jnp.where((j == 1) | (j == 4) | (j == 5) | (j == 7), other, core)
        return slot(d, k)

    def spread(ref, t, u):
        def copy(i):
            lo, hi = pl.ds(0, hn), pl.ds(hn, hn)
            twin = at_x(0, other)
            src, to = {
                0: (ref.at[u, col], at_x(1, core)),
                1: (ref.at[u, col], at_x(-1, core)),
                2: (ref.at[u, col], twin),
                3: (ref.at[u, slot(-1, core), lo], at_x(1, core)),
                4: (ref.at[u, slot(1, core), hi], at_x(-1, core)),
                5: (ref.at[u, slot(-1, core)], twin),
                6: (ref.at[u, slot(1, core)], twin),
                7: (ref.at[u, slot(2, core), lo], twin),
                8: (ref.at[u, slot(2, core), hi], twin),
            }[i]
            return rdesc(src, src, ug_s.at[t, u, i], ug_r.at[t, u, i], to)

        def begin():
            for i in range(3):
                copy(i).start()

        def middle():
            copy(0).wait_recv()
            copy(3).start()
            copy(5).start()
            copy(1).wait_recv()
            copy(4).start()
            copy(6).start()

        def finish():
            copy(3).wait_recv()
            copy(7).start()
            copy(4).wait_recv()
            copy(8).start()

        def got(*which):
            for i in which:
                copy(i).wait_recv()

        def close():
            for i in range(9):
                copy(i).wait_send()

        return begin, middle, finish, got, close

    tiles = ffd // 256

    def tile(j):
        return pl.ds(pl.multiple_of(j * 256, 256), 256)

    def rows_of(i, u, size):
        return pl.ds(pl.multiple_of(i * share + u * size, size), size)

    def target_block(fb, u):
        rows_at = pl.ds(pl.multiple_of(fb // 2 * m, m), m)
        lanes = pl.ds(pl.multiple_of(lax.rem(fb, 2) * share + u * half, half), half)
        return jnp.dot(p_ref[...], dbuf[rows_at, lanes], preferred_element_type=F32)

    t = tall(times_ref[...][None, :], n)

    def make_state(value, u):
        target = value.astype(BF16)
        target_ref[:, u * half : (u + 1) * half] = target
        target = target.astype(F32)
        noise = slopes[u, col].astype(F32)
        lanes = pl.ds(pl.multiple_of(col * share + u * half, half), half)
        st = (1.0 - t) * noise + t * target + t * embed_ref[:, lanes]
        latents[u, col] = (st * gain_ref[:, lanes]).astype(BF16)
        state[:, u * half : (u + 1) * half] = st - (target - noise)
        return jnp.sum(st * st, axis=1, keepdims=True)

    hb0, hm0, hf0, hg0, hc0 = spread(latents, 0, 0)
    hb1, hm1, hf1, hg1, hc1 = spread(latents, 0, 1)

    def target_half(u, _):
        when(u == 0, "t0")
        when(u == 1, "t2")
        cols_reduce(target_block, 0, u)
        return 0

    lax.fori_loop(0, 2, target_half, 0)
    at("t4")
    part = make_state(reduced(0, 0), 0)
    hb0()
    at("t5")
    part = part + make_state(reduced(0, 1), 1)
    part, _ = flat(part, part)
    rsend[ITERS, 0:1, :] = part
    rsend[ITERS, 1:2, :] = part
    cols_swap(ITERS)
    hm0()
    hb1()
    at("h0")
    hid[...] = jnp.zeros_like(hid)

    def hidden_step(j, _):
        @pl.when(j == 1)
        def _():
            at("h1")
            hf0()
            hm1()
            at("h2")
            hg0(2)
            hg1(2)

        @pl.when(j == 3)
        def _():
            hf1()

        @pl.when(j == 4)
        def _():
            at("h3")
            hg0(5)
            hg1(5)

        @pl.when(j == 5)
        def _():
            hg0(6)
            hg1(6)

        @pl.when(j == 7)
        def _():
            at("h4")
            hg0(7, 8)
            hg1(7, 8)

        i = visit(j)
        hid[...] += (jnp.dot(latents[0, i], win[rows_of(i, 0, half), :], preferred_element_type=F32)
                     + jnp.dot(latents[1, i], win[rows_of(i, 1, half), :], preferred_element_type=F32))
        return 0

    lax.fori_loop(0, n_cols, hidden_step, 0)
    hc0()
    hc1()
    await_all(rrecv.at[ITERS], rr.at[ITERS])
    await_all(rrecv.at[ITERS], rs.at[ITERS])
    square = part + jnp.sum(rrecv[ITERS][:, 0, :], axis=0, keepdims=True)
    scale = tall(lax.rsqrt(square / width + 1e-6), n)

    def gelu_step(j, _):
        h = hid[:, tile(j)] * scale
        c = math.sqrt(2.0 / math.pi)
        h2 = h * h
        th = jnp.tanh(c * (h + 0.044715 * (h2 * h)))
        act[:, tile(j)] = (0.5 * h * (1.0 + th)).astype(BF16)
        slope_of = 0.5 * (1.0 + th) + 0.5 * h * (1.0 - th * th) * (c * (1.0 + (3 * 0.044715) * h2))
        hid[:, tile(j)] = slope_of * scale
        return 0

    lax.fori_loop(0, tiles, gelu_step, 0)
    at("v0")

    def pair(ref, i, u, at):
        lo = ref[pl.ds(pl.multiple_of(i * share + u * eighth, eighth), eighth), at]
        hi = ref[pl.ds(pl.multiple_of(i * share + half + u * eighth, eighth), eighth), at]
        return jnp.concatenate([lo, hi], axis=0)

    def velocity_block(fb, u):
        return lax.dot_general(act[...], pair(wout, fb, u, slice(None)), NT, preferred_element_type=F32)

    def make_slope(value, u):
        lo = state[:, u * eighth : (u + 1) * eighth]
        hi = state[:, half + u * eighth : half + (u + 1) * eighth]
        slopes[u, col] = ((jnp.concatenate([lo, hi], axis=1) + value) * (1.0 / math.sqrt(tokens))).astype(BF16)

    TN = (((0,), (0,)), ((), ()))

    def use_slope(i, u):
        value = lax.dot_general(slopes[u, i], act[...], TN, preferred_element_type=F32).astype(BF16)
        dbuf[pl.ds(pl.multiple_of(i * share + u * eighth, eighth), eighth), :] = value[:eighth]
        dbuf[pl.ds(pl.multiple_of(i * share + half + u * eighth, eighth), eighth), :] = value[eighth:]

    def rx_at(ref, base, unit, path, j, part=None):
        high = unit[1]
        off = high // 2 if part == 1 else 0
        size = high if part is None else high // 2
        return ref.at[pl.ds(base + (path * 16 + j) * high + off, size)]

    def shift(w, path, i):
        ref = (dbuf, dbuf, win)[w]
        unit = (low, up, wide)[w]
        f, s = here(path)
        if i < 4:
            e, axis, d = (2, 1, 3, 0)[i], "f", 1 if i < 2 else -1
            src, dst = (f + 2, s + e, None), (i, None)
        elif i < 12:
            e, axis, d = i % 4, "f", 1 if i < 8 else -1
            src, dst = (f + d, s + e, None), (i, None)
        else:
            axis, d = "s", 1 if i % 2 == 0 else -1
            src, dst = {
                12: ((f, s + 2, 0), (12, 0)), 13: ((f, s + 2, 1), (12, 1)),
                14: ((f, s + 1, 1), (13, 1)), 15: ((f, s - 1, 0), (14, 0)),
                16: ((f, s + 1, 0), (13, 0)), 17: ((f, s - 1, 1), (14, 1)),
            }[i]
        return rdesc(piece(ref, unit, path, *src), landing(w, path, *dst),
                     gr_s.at[w, path, i], gr_r.at[w, path, i], toward(path, axis, d))

    def landing(w, path, j, part=None):
        return rx_at((rx, rx, wout)[w], (0, width // 2, 0)[w], (low, up, wide)[w], path, j, part)

    def add(at, *more):
        def rows_step(r, _):
            rows = pl.ds(pl.multiple_of(r * 32, 32), 32)
            value = at[rows, :].astype(F32)
            for one in more:
                value = value + one[rows, :].astype(F32)
            at[rows, :] = value.astype(BF16)
            return 0

        lax.fori_loop(0, at.shape[0] // 32, rows_step, 0)

    def scatter(w, step):
        ref = (dbuf, dbuf, win)[w]
        unit = (low, up, wide)[w]
        high = unit[1]
        if step == 1:
            for i in (0, 1, 2, 3, 4, 7, 9, 10):
                for path in range(2):
                    shift(w, path, i).start()
        for path in range(2):
            f, s = here(path)
            if step == 2:
                for j in range(2):
                    for d, i, e in ((1, j, (2, 1)[j]), (-1, 2 + j, (3, 0)[j])):
                        shift(w, path, i).wait_recv()
                        add(piece(ref, unit, path, f + d, s + e), landing(w, path, i))
                        shift(w, path, (4 if d == 1 else 8) + e).start()
            if step == 3:
                for e in ORDER:
                    shift(w, path, 4 + e).wait_recv()
                    shift(w, path, 8 + e).wait_recv()
                    add(piece(ref, unit, path, f, s + e), landing(w, path, 4 + e), landing(w, path, 8 + e))
                    for i in {2: (12, 13), 1: (14,), 3: (15,), 0: ()}[e]:
                        shift(w, path, i).start()
            if step == 4:
                shift(w, path, 12).wait_recv()
                add(piece(ref, unit, path, f, s + 1, 0), landing(w, path, 12, 0))
                shift(w, path, 16).start()
                shift(w, path, 13).wait_recv()
                add(piece(ref, unit, path, f, s - 1, 1), landing(w, path, 12, 1))
                shift(w, path, 17).start()
            if step == 5:
                for i in range(14, 18):
                    shift(w, path, i).wait_recv()
                value = (piece(ref, unit, path, f, s)[...].astype(F32) + landing(w, path, 13)[...].astype(F32)
                         + landing(w, path, 14)[...].astype(F32))
                if w < 2:
                    final[w, path * high : (path + 1) * high, :] = value
                    if path == 1:
                        gout_ref[:, w * 2 * high : (w + 1) * 2 * high] = final[w].T.astype(BF16)
                else:
                    gin_ref[path * high : (path + 1) * high, :] = value.astype(BF16)
                for i in range(18):
                    shift(w, path, i).wait_send()

    sb0, sm0, sf0, sg0, sc0 = spread(slopes, 1, 0)
    sb1, sm1, sf1, sg1, sc1 = spread(slopes, 1, 1)

    def velocity_half(u, _):
        when(u == 1, "v1")
        cols_reduce(velocity_block, 1, u)
        return 0

    lax.fori_loop(0, 2, velocity_half, 0)
    make_slope(reduced(1, 0), 0)
    sb0()

    def slope_step(jj, _):
        def on(number, *calls):
            @pl.when(jj == number)
            def _():
                for call in calls:
                    call()

        on(1, lambda: make_slope(reduced(1, 1), 1), sm0, sb1, lambda: sg0(2))
        on(4, sf0, lambda: sg0(5))
        on(5, lambda: sg0(6))
        on(7, lambda: sg0(7, 8))
        on(8, lambda: scatter(0, 1), sm1)
        on(9, lambda: sg1(2))
        on(12, sf1, lambda: sg1(5))
        on(13, lambda: sg1(6))
        on(15, lambda: sg1(7, 8))
        use_slope(visit(lax.rem(jj, 8)), jj // 8)
        return 0

    lax.fori_loop(0, 16, slope_step, 0)
    scatter(1, 1)
    sc0()
    sc1()
    scatter(0, 2)

    every = slice(None)
    back[...] = jnp.zeros_like(back)

    def back_step(i, _):
        back[...] += (jnp.dot(slopes[0, i], pair(wout, i, 0, every), preferred_element_type=F32)
                      + jnp.dot(slopes[1, i], pair(wout, i, 1, every), preferred_element_type=F32))
        return 0

    lax.fori_loop(0, n_cols, back_step, 0)
    for w in range(3):
        for path in range(2):
            for i in range(20):
                carry(w, path, i).wait_send()
    for path in range(2):
        for d in (1, -1):
            pl.semaphore_signal(credit, inc=1, device_id=toward(path, "f", d), device_id_type=MESH)
    scatter(1, 2)
    sh[...] = (back[...] * hid[...]).astype(BF16)

    def in_step(i, _):
        win[pl.ds(pl.multiple_of(i * half, half), half), :] = lax.dot_general(
            latents[lax.rem(i, 2), i // 2], sh[...], TN, preferred_element_type=F32).astype(BF16)
        return 0

    lax.fori_loop(0, 2 * n_cols, in_step, 0)
    pl.semaphore_wait(credit, 4)
    scatter(2, 1)
    scatter(0, 3)
    scatter(2, 2)
    scatter(1, 3)
    scatter(0, 4)
    scatter(2, 3)
    scatter(1, 4)
    scatter(2, 4)
    scatter(0, 5)
    scatter(1, 5)
    scatter(2, 5)


def hand_out(a, b, c, x, y, z, *rest):
    sem = rest[3]
    ins = [pltpu.make_async_copy(s, v, sem.at[i]) for i, (s, v) in enumerate(zip((a, b, c), rest))]
    outs = [pltpu.make_async_copy(v, d, sem.at[3 + i]) for i, (v, d) in enumerate(zip(rest, (x, y, z)))]
    for c in ins:
        c.start()
    for i in range(3):
        ins[i].wait()
        outs[i].start()
    for c in outs:
        c.wait()


def per_device(noise, data, times, time_embed, norm_gain, w_in, w_out):
    n, width = noise.shape
    m = data.shape[0]
    wr, ffd = w_in.shape
    share = width // 8
    half = share // 2
    vm = pl.BlockSpec(memory_space=pltpu.VMEM)
    hbm = pl.BlockSpec(memory_space=pl.ANY)
    dma = pltpu.SemaphoreType.DMA
    outs = pl.pallas_call(
        kernel,
        out_shape=(
            jax.ShapeDtypeStruct((n, share), BF16),
            jax.ShapeDtypeStruct((wr, ffd), BF16),
            jax.ShapeDtypeStruct((ffd, wr), BF16),
        ),
        in_specs=[hbm, hbm, vm, vm, vm, hbm, vm],
        out_specs=(vm, vm, vm),
        scratch_shapes=[
            pltpu.VMEM((2, 8, n, half), BF16),
            pltpu.VMEM((width, ffd), BF16),
            pltpu.VMEM((width, ffd), BF16),
            pltpu.VMEM((width, ffd), BF16),
            pltpu.VMEM((width, ffd), BF16),
            pltpu.VMEM((2, 8, n, half), BF16),
            pltpu.VMEM((n, ffd), BF16),
            pltpu.VMEM((n, ffd), F32),
            pltpu.VMEM((n, ffd), F32),
            pltpu.VMEM((n, m), F32),
            pltpu.VMEM((n, m), BF16),
            pltpu.VMEM((n, share), F32),
            pltpu.VMEM((n, ffd), BF16),
            pltpu.VMEM((2, 4, n, half), BF16),
            pltpu.VMEM((2, 4, n, half), BF16),
            pltpu.VMEM((2, 4, n, half), BF16),
            pltpu.VMEM((2, 2, n // 2, half), BF16),
            pltpu.VMEM((2, 2, n, half), BF16),
            pltpu.VMEM((2, n, half), F32),
            pltpu.VMEM((n, 128), F32),
            pltpu.VMEM((m, 128), F32),
            pltpu.VMEM((2, wr // 2, ffd), F32),
            pltpu.VMEM((ITERS, 2, m), F32),
            pltpu.VMEM((ITERS, 15, 2, m), F32),
            pltpu.VMEM((ITERS + 1, 2, n), F32),
            pltpu.VMEM((ITERS + 1, 7, 2, n), F32),
            dma((ITERS,)), dma((ITERS,)), dma((ITERS + 1,)), dma((ITERS + 1,)),
            dma((3, 2, 20)), dma((3, 2, 20)),
            dma((2, 2, 10)), dma((2, 2, 10)),
            dma((2, 2, 9)), dma((2, 2, 9)),
            dma((3, 2, 18)), dma((3, 2, 18)),
            dma((21,)),
            pltpu.SemaphoreType.REGULAR,
        ],
        compiler_params=pltpu.CompilerParams(
            collective_id=0, has_side_effects=True, vmem_limit_bytes=62 * 2**20
        ),
    )(noise, data, times, time_embed[None, :], norm_gain[None, :], w_in, w_out)
    return pl.pallas_call(
        hand_out,
        out_shape=tuple(jax.ShapeDtypeStruct(o.shape, o.dtype) for o in outs),
        in_specs=[hbm] * 3,
        out_specs=(hbm,) * 3,
        scratch_shapes=[pltpu.VMEM(o.shape, o.dtype) for o in outs] + [dma((6,))],
    )(*outs)


def solution(mesh):
    in_specs = (
        P("rows", None),
        P("cols", None),
        P("rows"),
        P(),
        P(),
        P("rows", "cols"),
        P("cols", "rows"),
    )
    out_specs = (P("rows", "cols"), P("rows", "cols"), P("cols", "rows"))
    return jax.shard_map(
        per_device, mesh=mesh, in_specs=in_specs, out_specs=out_specs, check_vma=False
    )
```

```python
import functools
import math

import jax
import jax.numpy as jnp
from jax import lax
from jax.experimental import pallas as pl
from jax.experimental.pallas import tpu as pltpu
from jax.sharding import PartitionSpec as P

ITERS = 3
EPSILON = 0.01
MESH = pl.DeviceIdType.MESH
F32 = jnp.float32
BF16 = jnp.bfloat16
NT = (((1,), (1,)), ((), ()))
ORDER = (2, 1, 3, 0)


def ring(value):
    return lax.rem(value + 4, 4)


def tall(row, rows):
    return jnp.broadcast_to(row, (128, rows)).T[:, 0:1]


def flat(left, right):
    lane = lax.broadcasted_iota(jnp.int32, (left.shape[0], 128), 1)
    both = jnp.where(lane < 64, left, right).T
    return both[0:1], both[64:65]


def kernel(noise_hbm, data_hbm, times_ref, embed_ref, gain_ref, w_in_hbm, w_out_ref,
           target_ref, gin_ref, gout_ref,
           slopes, dbuf, win, wout, rx, latents, act, hid, back, a_ref, p_ref, state, sh,
           sibs, sibr, outs, rh, rf, own, nsq, dsq, final,
           csend, crecv, rsend, rrecv,
           cs, cr, rs, rr, ag_s, ag_r, xs, xr, ug_s, ug_r, gr_s, gr_r, loc, credit):
    n_rows, n_cols = 16, 8
    row = lax.axis_index("rows")
    col = lax.axis_index("cols")
    z, y = row // 4, lax.rem(row, 4)
    xx, core = col // 2, lax.rem(col, 2)
    n, width = noise_hbm.shape
    m = data_hbm.shape[0]
    share = width // n_cols
    wr, ffd = w_in_hbm.shape
    half = share // 2
    eighth = share // 4
    hn = n // 2
    tokens = n * n_rows

    def rdesc(src, dst, send, recv, to):
        return pltpu.make_async_remote_copy(src_ref=src, dst_ref=dst, send_sem=send, recv_sem=recv,
                                            device_id=to, device_id_type=MESH)

    def rcopy(*args):
        rdesc(*args).start()

    barrier = pltpu.get_barrier_semaphore()
    for d in range(1, n_rows):
        pl.semaphore_signal(barrier, inc=1, device_id=(lax.rem(row + d, n_rows), col), device_id_type=MESH)
    for d in range(1, n_cols):
        pl.semaphore_signal(barrier, inc=1, device_id=(row, lax.rem(col + d, n_cols)), device_id_type=MESH)

    def mine(i):
        return pl.ds(pl.multiple_of(i * wr, wr), wr)

    w_copy = pltpu.make_async_copy(w_in_hbm, win.at[mine(row)], loc.at[0])
    w_copy.start()

    def noise_copy(q):
        return pltpu.make_async_copy(noise_hbm.at[:, pl.ds(pl.multiple_of(q * half, half), half)],
                                     slopes.at[lax.rem(q, 2), q // 2], loc.at[5 + q])

    def data_copy(q):
        return pltpu.make_async_copy(data_hbm.at[:, pl.ds(pl.multiple_of(q * 2 * share, 2 * share), 2 * share)],
                                     dbuf.at[pl.ds(pl.multiple_of(q * m, m), m)], loc.at[1 + q])

    for q in range(4):
        for h in range(4):
            noise_copy(4 * q + h).start()
        data_copy(q).start()
    wout[mine(row)] = w_out_ref[...].astype(F32).T.astype(BF16)
    w_copy.wait()

    def place(path, f, s):
        return s * 4 + f if path == 0 else f * 4 + s

    def here(path):
        return (y, z) if path == 0 else (z, y)

    def piece(ref, unit, path, f, s, part=None):
        base, high = unit
        off = base + path * high + (high // 2 if part == 1 else 0)
        size = high if part is None else high // 2
        return ref.at[pl.ds(pl.multiple_of(place(path, ring(f), ring(s)) * wr + off, high // 2), size)]

    wide, low, up = (0, wr // 2), (0, wr // 4), (wr // 2, wr // 4)

    def toward(path, axis, d):
        f, s = here(path)
        if axis == "f":
            return (place(path, ring(f + d), s), col)
        return (place(path, f, ring(s + d)), col)

    routes = [
        ("f", 1, 0, 0, None), ("f", -1, 0, 0, None), ("s", 1, 0, 0, None), ("s", -1, 0, 0, None),
        ("f", 1, -1, 0, 0), ("f", -1, 1, 0, 1),
        ("s", 1, -1, 0, None), ("s", -1, -1, 0, None), ("s", 1, 1, 0, None), ("s", -1, 1, 0, None),
        ("s", 1, 0, -1, 0), ("s", -1, 0, 1, 1), ("s", 1, 2, 0, None), ("s", -1, 2, 0, None),
        ("s", 1, -1, -1, 0), ("s", -1, -1, 1, 1), ("s", 1, 1, -1, 0), ("s", -1, 1, 1, 1),
        ("s", 1, 2, -1, 0), ("s", -1, 2, 1, 1),
    ]

    def carry(w, path, i):
        axis, d, df, ds_, part = routes[i]
        f, s = here(path)
        spot = piece((win, wout, wout)[w], (wide, low, up)[w], path, f + df, s + ds_, part)
        return rdesc(spot, spot, ag_s.at[w, path, i], ag_r.at[w, path, i], toward(path, axis, d))

    sends = {"1": (0, 1, 2, 3), "2a": (4, 5, 6, 7, 8, 9), "2b": (10, 11), "3a": (12, 13), "3b": (14, 15),
             "3c": (16, 17), "4": (18, 19), "2x": (4, 5, 6, 7), "2y": (8, 9, 10, 11), "3x": (12, 13, 14, 15)}
    needs = {"2x": (0, 1), "2y": (2, 3), "3x": (4, 5, 6, 7), "2a": (0, 1), "2b": (2, 3), "3a": (4, 5), "3b": (6, 7), "3c": (8, 9), "4": (12, 13),
             "end": (10, 11, 14, 15, 16, 17, 18, 19)}

    def gather(w, *steps):
        for step in steps:
            for i in needs.get(step, ()):
                for path in range(2):
                    carry(w, path, i).wait_recv()
            for i in sends.get(step, ()):
                for path in range(2):
                    carry(w, path, i).start()

    plan = {
        "p0": [(0,"1"), (1,"1")],
        "k0c": [(0,"2x")],
        "k1c": [(0,"2y")],
        "k2c": [(0,"3x")],
        "t0": [(0,"3c"), (2,"1")],
        "t2": [(0,"4"), (1,"2a","2b")],
        "t4": [(2,"2x")],
        "h0": [(0,"end"), (1,"3a","3b","3c"), (2,"2y")],
        "h2": [(1,"4")],
        "h3": [(2,"3x")],
        "h4": [(2,"3c")],
        "v0": [(2,"4"), (1,"end")],
        "v1": [(2,"end")],
    }

    def at(point):
        for job in plan.get(point, ()):
            gather(*job)

    pl.semaphore_wait(barrier, n_rows + n_cols - 2)
    at("p0")

    def squares(value):
        value = value.astype(F32)
        value = value * value
        out = value[:, 0:128]
        for j in range(1, value.shape[1] // 128):
            out = out + value[:, j * 128 : (j + 1) * 128]
        return out

    a_ref[...] = jnp.zeros_like(a_ref)
    nsq[...] = jnp.zeros_like(nsq)
    dsq[...] = jnp.zeros_like(dsq)

    def cost_step(q, _):
        for h in range(4):
            noise_copy(4 * q + h).wait()
        data_copy(q).wait()
        total = None
        for h in range(4):
            term = lax.dot_general(slopes[h % 2, 2 * q + h // 2],
                                   dbuf[pl.ds(pl.multiple_of(q * m, m), m), h * half : (h + 1) * half], NT,
                                   preferred_element_type=F32)
            total = term if total is None else total + term
        a_ref[...] += total

        def noise_rows(i, _):
            at = pl.ds(pl.multiple_of(i * 32, 32), 32)
            value = squares(slopes[0, 2 * q, at, :])
            for h in range(1, 4):
                value = value + squares(slopes[h % 2, 2 * q + h // 2, at, :])
            nsq[at, :] += value
            return 0

        def data_rows(i, _):
            at = pl.ds(pl.multiple_of(i * 32, 32), 32)
            dsq[at, :] += squares(dbuf[pl.ds(pl.multiple_of(q * m + i * 32, 32), 32), :])
            return 0

        lax.fori_loop(0, n // 32, noise_rows, 0)
        lax.fori_loop(0, m // 32, data_rows, 0)
        return 0

    lax.fori_loop(0, 4, cost_step, 0)
    noise_sq = jnp.sum(nsq[...], axis=1, keepdims=True)
    data_sq = jnp.sum(dsq[...].T, axis=0, keepdims=True)
    a_ref[...] = (noise_sq + data_sq - 2.0 * a_ref[...]) * (1.0 / (width * EPSILON))
    base = -math.log(tokens)
    at("c4")

    def rows_swap(it):
        for d in range(1, n_rows):
            rcopy(csend.at[it], crecv.at[it, d - 1], cs.at[it], cr.at[it], (lax.rem(row + d, n_rows), col))

    def cols_swap(it):
        for d in range(1, n_cols):
            rcopy(rsend.at[it], rrecv.at[it, d - 1], rs.at[it], rr.at[it], (row, lax.rem(col + d, n_cols)))

    def await_all(ref, sem):
        pltpu.make_async_copy(ref, ref, sem).wait()

    def merge(got, top, tot):
        gt = got[:, 0, :]
        best = jnp.maximum(top, jnp.max(gt, axis=0, keepdims=True))
        total = tot * jnp.exp(top - best) + jnp.sum(got[:, 1, :] * jnp.exp(gt - best), axis=0, keepdims=True)
        return base - (best + jnp.log(total))

    def when(condition, *points):
        @pl.when(condition)
        def _():
            for point in points:
                at(point)

    def sweep(it, fg):
        x = fg[0] - a_ref[...]
        top = jnp.max(x, axis=0, keepdims=True)
        tot = jnp.sum(jnp.exp(x - top), axis=0, keepdims=True)
        csend[it, 0:1, :] = top
        csend[it, 1:2, :] = tot
        rows_swap(it)
        for i in range(ITERS):
            when(it == i, ("k0c", "k1c", "k2c")[i])
        await_all(crecv.at[it], cr.at[it])
        g = merge(crecv[it], top, tot)

        x = g - a_ref[...]
        top = jnp.max(x, axis=1, keepdims=True)
        tot = jnp.sum(jnp.exp(x - top), axis=1, keepdims=True)
        top, tot = flat(top, tot)
        rsend[it, 0:1, :] = top
        rsend[it, 1:2, :] = tot
        cols_swap(it)
        for i in range(ITERS):
            when(it == i, ("k0r", "k1r", "k2r")[i])
        await_all(rrecv.at[it], rr.at[it])
        return tall(merge(rrecv[it], top, tot), n), g

    f, g = lax.fori_loop(0, ITERS, sweep, (jnp.zeros((n, 1), F32), jnp.zeros((1, m), F32)))
    p_ref[...] = (float(tokens) * jnp.exp(f + g - a_ref[...])).astype(BF16)
    for it in range(ITERS):
        await_all(crecv.at[it], cs.at[it])
        await_all(rrecv.at[it], rs.at[it])

    def at_x(d, k):
        return (row, ring(xx + d) * 2 + k)

    def reduce_copy(t, u, i):
        lo, hi = pl.ds(0, hn), pl.ds(hn, hn)
        if not isinstance(i, int):
            src, dst, to = sibs.at[u, i], sibr.at[u, i], at_x(0, 1 - core)
        else:
            src, dst, d = {
                4: (outs.at[u, 0, lo], rh.at[u, 0], 1),
                5: (outs.at[u, 0, hi], rh.at[u, 1], -1),
                6: (outs.at[u, 1, hi], rf.at[u, 0, hi], 1),
                7: (outs.at[u, 2, lo], rf.at[u, 1, lo], -1),
                8: (outs.at[u, 1, lo], rf.at[u, 0, lo], 1),
                9: (outs.at[u, 2, hi], rf.at[u, 1, hi], -1),
            }[i]
            to = at_x(d, core)
        return rdesc(src, dst, xs.at[t, u, i], xr.at[t, u, i], to)

    def cols_reduce(make, t, u):
        def offset(i):
            return jnp.where(i == 0, 2, jnp.where(i == 3, 0, 2 * i - 1))

        def twin_step(i, _):
            sibs[u, i] = make(ring(xx + offset(i)) * 2 + 1 - core, u).astype(BF16)
            reduce_copy(t, u, i).start()
            return 0

        def block_step(i, _):
            d = offset(i)
            value = make(ring(xx + d) * 2 + core, u)
            reduce_copy(t, u, i).wait_recv()
            value = value + sibr[u, i].astype(F32)
            own[u] = value
            outs[u, i] = value.astype(BF16)

            @pl.when(i == 0)
            def _():
                reduce_copy(t, u, 4).start()
                reduce_copy(t, u, 5).start()

            @pl.when(i == 1)
            def _():
                reduce_copy(t, u, 6).start()

            @pl.when(i == 2)
            def _():
                reduce_copy(t, u, 7).start()

            return 0

        lax.fori_loop(0, 4, twin_step, 0)
        lax.fori_loop(0, 4, block_step, 0)
        reduce_copy(t, u, 4).wait_recv()
        outs[u, 1, 0:hn] = (outs[u, 1, 0:hn].astype(F32) + rh[u, 0].astype(F32)).astype(BF16)
        reduce_copy(t, u, 8).start()
        reduce_copy(t, u, 5).wait_recv()
        outs[u, 2, hn:n] = (outs[u, 2, hn:n].astype(F32) + rh[u, 1].astype(F32)).astype(BF16)
        reduce_copy(t, u, 9).start()

    def reduced(t, u):
        for i in (6, 7, 8, 9):
            reduce_copy(t, u, i).wait_recv()
        value = own[u] + rf[u, 0].astype(F32) + rf[u, 1].astype(F32)
        for i in range(4):
            reduce_copy(t, u, jnp.int32(i)).wait_send()
        for i in range(4, 10):
            reduce_copy(t, u, i).wait_send()
        return value

    def slot(d, k):
        return ring(xx + d) * 2 + k

    other = 1 - core

    def visit(j):
        d = jnp.where(j < 2, 0, jnp.where(j >= 6, 2, 2 * lax.rem(j, 2) - 1))
        k = jnp.where((j == 1) | (j == 4) | (j == 5) | (j == 7), other, core)
        return slot(d, k)

    def spread(ref, t, u):
        def copy(i):
            lo, hi = pl.ds(0, hn), pl.ds(hn, hn)
            twin = at_x(0, other)
            src, to = {
                0: (ref.at[u, col], at_x(1, core)),
                1: (ref.at[u, col], at_x(-1, core)),
                2: (ref.at[u, col], twin),
                3: (ref.at[u, slot(-1, core), lo], at_x(1, core)),
                4: (ref.at[u, slot(1, core), hi], at_x(-1, core)),
                5: (ref.at[u, slot(-1, core)], twin),
                6: (ref.at[u, slot(1, core)], twin),
                7: (ref.at[u, slot(2, core), lo], twin),
                8: (ref.at[u, slot(2, core), hi], twin),
            }[i]
            return rdesc(src, src, ug_s.at[t, u, i], ug_r.at[t, u, i], to)

        def begin():
            for i in range(3):
                copy(i).start()

        def middle():
            copy(0).wait_recv()
            copy(3).start()
            copy(5).start()
            copy(1).wait_recv()
            copy(4).start()
            copy(6).start()

        def finish():
            copy(3).wait_recv()
            copy(7).start()
            copy(4).wait_recv()
            copy(8).start()

        def got(*which):
            for i in which:
                copy(i).wait_recv()

        def close():
            for i in range(9):
                copy(i).wait_send()

        return begin, middle, finish, got, close

    tiles = ffd // 256

    def tile(j):
        return pl.ds(pl.multiple_of(j * 256, 256), 256)

    def rows_of(i, u, size):
        return pl.ds(pl.multiple_of(i * share + u * size, size), size)

    def target_block(fb, u):
        rows_at = pl.ds(pl.multiple_of(fb // 2 * m, m), m)
        lanes = pl.ds(pl.multiple_of(lax.rem(fb, 2) * share + u * half, half), half)
        return jnp.dot(p_ref[...], dbuf[rows_at, lanes], preferred_element_type=F32)

    t = tall(times_ref[...][None, :], n)

    def make_state(value, u):
        target = value.astype(BF16)
        target_ref[:, u * half : (u + 1) * half] = target
        target = target.astype(F32)
        noise = slopes[u, col].astype(F32)
        lanes = pl.ds(pl.multiple_of(col * share + u * half, half), half)
        st = (1.0 - t) * noise + t * target + t * embed_ref[:, lanes]
        latents[u, col] = (st * gain_ref[:, lanes]).astype(BF16)
        state[:, u * half : (u + 1) * half] = st - (target - noise)
        return jnp.sum(st * st, axis=1, keepdims=True)

    hb0, hm0, hf0, hg0, hc0 = spread(latents, 0, 0)
    hb1, hm1, hf1, hg1, hc1 = spread(latents, 0, 1)

    def target_half(u, _):
        when(u == 0, "t0")
        when(u == 1, "t2")
        cols_reduce(target_block, 0, u)
        return 0

    lax.fori_loop(0, 2, target_half, 0)
    at("t4")
    part = make_state(reduced(0, 0), 0)
    hb0()
    at("t5")
    part = part + make_state(reduced(0, 1), 1)
    part, _ = flat(part, part)
    rsend[ITERS, 0:1, :] = part
    rsend[ITERS, 1:2, :] = part
    cols_swap(ITERS)
    hm0()
    hb1()
    at("h0")
    hid[...] = jnp.zeros_like(hid)

    def hidden_step(j, _):
        @pl.when(j == 1)
        def _():
            at("h1")
            hf0()
            hm1()
            at("h2")
            hg0(2)
            hg1(2)

        @pl.when(j == 3)
        def _():
            hf1()

        @pl.when(j == 4)
        def _():
            at("h3")
            hg0(5)
            hg1(5)

        @pl.when(j == 5)
        def _():
            hg0(6)
            hg1(6)

        @pl.when(j == 7)
        def _():
            at("h4")
            hg0(7, 8)
            hg1(7, 8)

        i = visit(j)
        hid[...] += (jnp.dot(latents[0, i], win[rows_of(i, 0, half), :], preferred_element_type=F32)
                     + jnp.dot(latents[1, i], win[rows_of(i, 1, half), :], preferred_element_type=F32))
        return 0

    lax.fori_loop(0, n_cols, hidden_step, 0)
    hc0()
    hc1()
    await_all(rrecv.at[ITERS], rr.at[ITERS])
    await_all(rrecv.at[ITERS], rs.at[ITERS])
    square = part + jnp.sum(rrecv[ITERS][:, 0, :], axis=0, keepdims=True)
    scale = tall(lax.rsqrt(square / width + 1e-6), n)

    def gelu_step(j, _):
        h = hid[:, tile(j)] * scale
        c = math.sqrt(2.0 / math.pi)
        h2 = h * h
        th = jnp.tanh(c * (h + 0.044715 * (h2 * h)))
        act[:, tile(j)] = (0.5 * h * (1.0 + th)).astype(BF16)
        slope_of = 0.5 * (1.0 + th) + 0.5 * h * (1.0 - th * th) * (c * (1.0 + (3 * 0.044715) * h2))
        hid[:, tile(j)] = slope_of * scale
        return 0

    lax.fori_loop(0, tiles, gelu_step, 0)
    at("v0")

    def pair(ref, i, u, at):
        lo = ref[pl.ds(pl.multiple_of(i * share + u * eighth, eighth), eighth), at]
        hi = ref[pl.ds(pl.multiple_of(i * share + half + u * eighth, eighth), eighth), at]
        return jnp.concatenate([lo, hi], axis=0)

    def velocity_block(fb, u):
        return lax.dot_general(act[...], pair(wout, fb, u, slice(None)), NT, preferred_element_type=F32)

    def make_slope(value, u):
        lo = state[:, u * eighth : (u + 1) * eighth]
        hi = state[:, half + u * eighth : half + (u + 1) * eighth]
        slopes[u, col] = ((jnp.concatenate([lo, hi], axis=1) + value) * (1.0 / math.sqrt(tokens))).astype(BF16)

    TN = (((0,), (0,)), ((), ()))

    def use_slope(i, u):
        value = lax.dot_general(slopes[u, i], act[...], TN, preferred_element_type=F32).astype(BF16)
        dbuf[pl.ds(pl.multiple_of(i * share + u * eighth, eighth), eighth), :] = value[:eighth]
        dbuf[pl.ds(pl.multiple_of(i * share + half + u * eighth, eighth), eighth), :] = value[eighth:]

    def rx_at(ref, base, unit, path, j, part=None):
        high = unit[1]
        off = high // 2 if part == 1 else 0
        size = high if part is None else high // 2
        return ref.at[pl.ds(base + (path * 16 + j) * high + off, size)]

    def shift(w, path, i):
        ref = (dbuf, dbuf, win)[w]
        unit = (low, up, wide)[w]
        f, s = here(path)
        if i < 4:
            e, axis, d = (2, 1, 3, 0)[i], "f", 1 if i < 2 else -1
            src, dst = (f + 2, s + e, None), (i, None)
        elif i < 12:
            e, axis, d = i % 4, "f", 1 if i < 8 else -1
            src, dst = (f + d, s + e, None), (i, None)
        else:
            axis, d = "s", 1 if i % 2 == 0 else -1
            src, dst = {
                12: ((f, s + 2, 0), (12, 0)), 13: ((f, s + 2, 1), (12, 1)),
                14: ((f, s + 1, 1), (13, 1)), 15: ((f, s - 1, 0), (14, 0)),
                16: ((f, s + 1, 0), (13, 0)), 17: ((f, s - 1, 1), (14, 1)),
            }[i]
        return rdesc(piece(ref, unit, path, *src), landing(w, path, *dst),
                     gr_s.at[w, path, i], gr_r.at[w, path, i], toward(path, axis, d))

    def landing(w, path, j, part=None):
        return rx_at((rx, rx, wout)[w], (0, width // 2, 0)[w], (low, up, wide)[w], path, j, part)

    def add(at, *more):
        def rows_step(r, _):
            rows = pl.ds(pl.multiple_of(r * 32, 32), 32)
            value = at[rows, :].astype(F32)
            for one in more:
                value = value + one[rows, :].astype(F32)
            at[rows, :] = value.astype(BF16)
            return 0

        lax.fori_loop(0, at.shape[0] // 32, rows_step, 0)

    def scatter(w, step):
        ref = (dbuf, dbuf, win)[w]
        unit = (low, up, wide)[w]
        high = unit[1]
        if step == 1:
            for i in (0, 1, 2, 3, 4, 7, 9, 10):
                for path in range(2):
                    shift(w, path, i).start()
        for path in range(2):
            f, s = here(path)
            if step == 2:
                for j in range(2):
                    for d, i, e in ((1, j, (2, 1)[j]), (-1, 2 + j, (3, 0)[j])):
                        shift(w, path, i).wait_recv()
                        add(piece(ref, unit, path, f + d, s + e), landing(w, path, i))
                        shift(w, path, (4 if d == 1 else 8) + e).start()
            if step == 3:
                for e in ORDER:
                    shift(w, path, 4 + e).wait_recv()
                    shift(w, path, 8 + e).wait_recv()
                    add(piece(ref, unit, path, f, s + e), landing(w, path, 4 + e), landing(w, path, 8 + e))
                    for i in {2: (12, 13), 1: (14,), 3: (15,), 0: ()}[e]:
                        shift(w, path, i).start()
            if step == 4:
                shift(w, path, 12).wait_recv()
                add(piece(ref, unit, path, f, s + 1, 0), landing(w, path, 12, 0))
                shift(w, path, 16).start()
                shift(w, path, 13).wait_recv()
                add(piece(ref, unit, path, f, s - 1, 1), landing(w, path, 12, 1))
                shift(w, path, 17).start()
            if step == 5:
                for i in range(14, 18):
                    shift(w, path, i).wait_recv()
                value = (piece(ref, unit, path, f, s)[...].astype(F32) + landing(w, path, 13)[...].astype(F32)
                         + landing(w, path, 14)[...].astype(F32))
                if w < 2:
                    final[w, path * high : (path + 1) * high, :] = value
                    if path == 1:
                        gout_ref[:, w * 2 * high : (w + 1) * 2 * high] = final[w].T.astype(BF16)
                else:
                    gin_ref[path * high : (path + 1) * high, :] = value.astype(BF16)
                for i in range(18):
                    shift(w, path, i).wait_send()

    sb0, sm0, sf0, sg0, sc0 = spread(slopes, 1, 0)
    sb1, sm1, sf1, sg1, sc1 = spread(slopes, 1, 1)

    def velocity_half(u, _):
        when(u == 1, "v1")
        cols_reduce(velocity_block, 1, u)
        return 0

    lax.fori_loop(0, 2, velocity_half, 0)
    make_slope(reduced(1, 0), 0)
    sb0()

    def slope_step(jj, _):
        def on(number, *calls):
            @pl.when(jj == number)
            def _():
                for call in calls:
                    call()

        on(1, lambda: make_slope(reduced(1, 1), 1), sm0, sb1, lambda: sg0(2))
        on(4, sf0, lambda: sg0(5))
        on(5, lambda: sg0(6))
        on(7, lambda: sg0(7, 8))
        on(8, lambda: scatter(0, 1), sm1)
        on(9, lambda: sg1(2))
        on(12, sf1, lambda: sg1(5))
        on(13, lambda: sg1(6))
        on(15, lambda: sg1(7, 8))
        use_slope(visit(lax.rem(jj, 8)), jj // 8)
        return 0

    lax.fori_loop(0, 16, slope_step, 0)
    scatter(1, 1)
    sc0()
    sc1()
    scatter(0, 2)

    every = slice(None)
    back[...] = jnp.zeros_like(back)

    def back_step(i, _):
        back[...] += (jnp.dot(slopes[0, i], pair(wout, i, 0, every), preferred_element_type=F32)
                      + jnp.dot(slopes[1, i], pair(wout, i, 1, every), preferred_element_type=F32))
        return 0

    lax.fori_loop(0, n_cols, back_step, 0)
    for w in range(3):
        for path in range(2):
            for i in range(20):
                carry(w, path, i).wait_send()
    for path in range(2):
        for d in (1, -1):
            pl.semaphore_signal(credit, inc=1, device_id=toward(path, "f", d), device_id_type=MESH)
    scatter(1, 2)
    sh[...] = (back[...] * hid[...]).astype(BF16)

    def in_step(i, _):
        win[pl.ds(pl.multiple_of(i * half, half), half), :] = lax.dot_general(
            latents[lax.rem(i, 2), i // 2], sh[...], TN, preferred_element_type=F32).astype(BF16)
        return 0

    lax.fori_loop(0, 2 * n_cols, in_step, 0)
    pl.semaphore_wait(credit, 4)
    scatter(2, 1)
    scatter(0, 3)
    scatter(2, 2)
    scatter(1, 3)
    scatter(0, 4)
    scatter(2, 3)
    scatter(1, 4)
    scatter(2, 4)
    scatter(0, 5)
    scatter(1, 5)
    scatter(2, 5)


def hand_out(a, b, c, x, y, z, *rest):
    sem = rest[3]
    ins = [pltpu.make_async_copy(s, v, sem.at[i]) for i, (s, v) in enumerate(zip((a, b, c), rest))]
    outs = [pltpu.make_async_copy(v, d, sem.at[3 + i]) for i, (v, d) in enumerate(zip(rest, (x, y, z)))]
    for c in ins:
        c.start()
    for i in range(3):
        ins[i].wait()
        outs[i].start()
    for c in outs:
        c.wait()


def per_device(noise, data, times, time_embed, norm_gain, w_in, w_out):
    n, width = noise.shape
    m = data.shape[0]
    wr, ffd = w_in.shape
    share = width // 8
    half = share // 2
    vm = pl.BlockSpec(memory_space=pltpu.VMEM)
    hbm = pl.BlockSpec(memory_space=pl.ANY)
    dma = pltpu.SemaphoreType.DMA
    outs = pl.pallas_call(
        kernel,
        out_shape=(
            jax.ShapeDtypeStruct((n, share), BF16),
            jax.ShapeDtypeStruct((wr, ffd), BF16),
            jax.ShapeDtypeStruct((ffd, wr), BF16),
        ),
        in_specs=[hbm, hbm, vm, vm, vm, hbm, vm],
        out_specs=(vm, vm, vm),
        scratch_shapes=[
            pltpu.VMEM((2, 8, n, half), BF16),
            pltpu.VMEM((width, ffd), BF16),
            pltpu.VMEM((width, ffd), BF16),
            pltpu.VMEM((width, ffd), BF16),
            pltpu.VMEM((width, ffd), BF16),
            pltpu.VMEM((2, 8, n, half), BF16),
            pltpu.VMEM((n, ffd), BF16),
            pltpu.VMEM((n, ffd), F32),
            pltpu.VMEM((n, ffd), F32),
            pltpu.VMEM((n, m), F32),
            pltpu.VMEM((n, m), BF16),
            pltpu.VMEM((n, share), F32),
            pltpu.VMEM((n, ffd), BF16),
            pltpu.VMEM((2, 4, n, half), BF16),
            pltpu.VMEM((2, 4, n, half), BF16),
            pltpu.VMEM((2, 4, n, half), BF16),
            pltpu.VMEM((2, 2, n // 2, half), BF16),
            pltpu.VMEM((2, 2, n, half), BF16),
            pltpu.VMEM((2, n, half), F32),
            pltpu.VMEM((n, 128), F32),
            pltpu.VMEM((m, 128), F32),
            pltpu.VMEM((2, wr // 2, ffd), F32),
            pltpu.VMEM((ITERS, 2, m), F32),
            pltpu.VMEM((ITERS, 15, 2, m), F32),
            pltpu.VMEM((ITERS + 1, 2, n), F32),
            pltpu.VMEM((ITERS + 1, 7, 2, n), F32),
            dma((ITERS,)), dma((ITERS,)), dma((ITERS + 1,)), dma((ITERS + 1,)),
            dma((3, 2, 20)), dma((3, 2, 20)),
            dma((2, 2, 10)), dma((2, 2, 10)),
            dma((2, 2, 9)), dma((2, 2, 9)),
            dma((3, 2, 18)), dma((3, 2, 18)),
            dma((21,)),
            pltpu.SemaphoreType.REGULAR,
        ],
        compiler_params=pltpu.CompilerParams(
            collective_id=0, has_side_effects=True, vmem_limit_bytes=62 * 2**20
        ),
    )(noise, data, times, time_embed[None, :], norm_gain[None, :], w_in, w_out)
    return pl.pallas_call(
        hand_out,
        out_shape=tuple(jax.ShapeDtypeStruct(o.shape, o.dtype) for o in outs),
        in_specs=[hbm] * 3,
        out_specs=(hbm,) * 3,
        scratch_shapes=[pltpu.VMEM(o.shape, o.dtype) for o in outs] + [dma((6,))],
    )(*outs)


def solution(mesh):
    in_specs = (
        P("rows", None),
        P("cols", None),
        P("rows"),
        P(),
        P(),
        P("rows", "cols"),
        P("cols", "rows"),
    )
    out_specs = (P("rows", "cols"), P("rows", "cols"), P("cols", "rows"))
    return jax.shard_map(
        per_device, mesh=mesh, in_specs=in_specs, out_specs=out_specs, check_vma=False
    )
```

```python
import functools
import math

import jax
import jax.numpy as jnp
from jax import lax
from jax.experimental import pallas as pl
from jax.experimental.pallas import tpu as pltpu
from jax.sharding import PartitionSpec as P

ITERS = 3
EPSILON = 0.01
MESH = pl.DeviceIdType.MESH
F32 = jnp.float32
BF16 = jnp.bfloat16
NT = (((1,), (1,)), ((), ()))
ORDER = (2, 1, 3, 0)


def ring(value):
    return lax.rem(value + 4, 4)


def tall(row, rows):
    return jnp.broadcast_to(row, (128, rows)).T[:, 0:1]


def flat(left, right):
    lane = lax.broadcasted_iota(jnp.int32, (left.shape[0], 128), 1)
    both = jnp.where(lane < 64, left, right).T
    return both[0:1], both[64:65]


def kernel(noise_hbm, data_hbm, times_ref, embed_ref, gain_ref, w_in_hbm, w_out_ref,
           target_ref, gin_ref, gout_ref,
           slopes, dbuf, win, wout, rx, latents, act, hid, back, a_ref, p_ref, state, sh,
           sibs, sibr, outs, rh, rf, own, nsq, dsq, final,
           csend, crecv, rsend, rrecv,
           cs, cr, rs, rr, ag_s, ag_r, xs, xr, ug_s, ug_r, gr_s, gr_r, loc, credit):
    n_rows, n_cols = 16, 8
    row = lax.axis_index("rows")
    col = lax.axis_index("cols")
    z, y = row // 4, lax.rem(row, 4)
    xx, core = col // 2, lax.rem(col, 2)
    n, width = noise_hbm.shape
    m = data_hbm.shape[0]
    share = width // n_cols
    wr, ffd = w_in_hbm.shape
    half = share // 2
    eighth = share // 4
    hn = n // 2
    tokens = n * n_rows

    def rdesc(src, dst, send, recv, to):
        return pltpu.make_async_remote_copy(src_ref=src, dst_ref=dst, send_sem=send, recv_sem=recv,
                                            device_id=to, device_id_type=MESH)

    def rcopy(*args):
        rdesc(*args).start()

    barrier = pltpu.get_barrier_semaphore()
    for d in range(1, n_rows):
        pl.semaphore_signal(barrier, inc=1, device_id=(lax.rem(row + d, n_rows), col), device_id_type=MESH)
    for d in range(1, n_cols):
        pl.semaphore_signal(barrier, inc=1, device_id=(row, lax.rem(col + d, n_cols)), device_id_type=MESH)

    def mine(i):
        return pl.ds(pl.multiple_of(i * wr, wr), wr)

    w_copy = pltpu.make_async_copy(w_in_hbm, win.at[mine(row)], loc.at[0])
    w_copy.start()

    def noise_copy(q):
        return pltpu.make_async_copy(noise_hbm.at[:, pl.ds(pl.multiple_of(q * half, half), half)],
                                     slopes.at[lax.rem(q, 2), q // 2], loc.at[5 + q])

    def data_copy(q):
        return pltpu.make_async_copy(data_hbm.at[:, pl.ds(pl.multiple_of(q * 2 * share, 2 * share), 2 * share)],
                                     dbuf.at[pl.ds(pl.multiple_of(q * m, m), m)], loc.at[1 + q])

    for q in range(4):
        for h in range(4):
            noise_copy(4 * q + h).start()
        data_copy(q).start()
    wout[mine(row)] = w_out_ref[...].astype(F32).T.astype(BF16)
    w_copy.wait()

    def place(path, f, s):
        return s * 4 + f if path == 0 else f * 4 + s

    def here(path):
        return (y, z) if path == 0 else (z, y)

    def piece(ref, unit, path, f, s, part=None):
        base, high = unit
        off = base + path * high + (high // 2 if part == 1 else 0)
        size = high if part is None else high // 2
        return ref.at[pl.ds(pl.multiple_of(place(path, ring(f), ring(s)) * wr + off, high // 2), size)]

    wide, low, up = (0, wr // 2), (0, wr // 4), (wr // 2, wr // 4)

    def toward(path, axis, d):
        f, s = here(path)
        if axis == "f":
            return (place(path, ring(f + d), s), col)
        return (place(path, f, ring(s + d)), col)

    routes = [
        ("f", 1, 0, 0, None), ("f", -1, 0, 0, None), ("s", 1, 0, 0, None), ("s", -1, 0, 0, None),
        ("f", 1, -1, 0, 0), ("f", -1, 1, 0, 1),
        ("s", 1, -1, 0, None), ("s", -1, -1, 0, None), ("s", 1, 1, 0, None), ("s", -1, 1, 0, None),
        ("s", 1, 0, -1, 0), ("s", -1, 0, 1, 1), ("s", 1, 2, 0, None), ("s", -1, 2, 0, None),
        ("s", 1, -1, -1, 0), ("s", -1, -1, 1, 1), ("s", 1, 1, -1, 0), ("s", -1, 1, 1, 1),
        ("s", 1, 2, -1, 0), ("s", -1, 2, 1, 1),
    ]

    def carry(w, path, i):
        axis, d, df, ds_, part = routes[i]
        f, s = here(path)
        spot = piece((win, wout, wout)[w], (wide, low, up)[w], path, f + df, s + ds_, part)
        return rdesc(spot, spot, ag_s.at[w, path, i], ag_r.at[w, path, i], toward(path, axis, d))

    sends = {"1": (0, 1, 2, 3), "2a": (4, 5, 6, 7, 8, 9), "2b": (10, 11), "3a": (12, 13), "3b": (14, 15),
             "3c": (16, 17), "4": (18, 19), "2x": (4, 5, 6, 7), "2y": (8, 9, 10, 11), "3x": (12, 13, 14, 15)}
    needs = {"2x": (0, 1), "2y": (2, 3), "3x": (4, 5, 6, 7), "2a": (0, 1), "2b": (2, 3), "3a": (4, 5), "3b": (6, 7), "3c": (8, 9), "4": (12, 13),
             "end": (10, 11, 14, 15, 16, 17, 18, 19)}

    def gather(w, *steps):
        for step in steps:
            for i in needs.get(step, ()):
                for path in range(2):
                    carry(w, path, i).wait_recv()
            for i in sends.get(step, ()):
                for path in range(2):
                    carry(w, path, i).start()

    plan = {
        "p0": [(0,"1"), (1,"1")],
        "k0c": [(0,"2x")],
        "k1c": [(0,"2y")],
        "k2c": [(0,"3x")],
        "t0": [(0,"3c"), (2,"1")],
        "t2": [(0,"4"), (1,"2a","2b")],
        "t4": [(2,"2x")],
        "h0": [(0,"end"), (1,"3a","3b","3c"), (2,"2y")],
        "h2": [(1,"4")],
        "h3": [(2,"3x")],
        "h4": [(2,"3c")],
        "v0": [(2,"4"), (1,"end")],
        "v1": [(2,"end")],
    }

    def at(point):
        for job in plan.get(point, ()):
            gather(*job)

    pl.semaphore_wait(barrier, n_rows + n_cols - 2)
    at("p0")

    def squares(value):
        value = value.astype(F32)
        value = value * value
        out = value[:, 0:128]
        for j in range(1, value.shape[1] // 128):
            out = out + value[:, j * 128 : (j + 1) * 128]
        return out

    a_ref[...] = jnp.zeros_like(a_ref)
    nsq[...] = jnp.zeros_like(nsq)
    dsq[...] = jnp.zeros_like(dsq)

    def cost_step(q, _):
        for h in range(4):
            noise_copy(4 * q + h).wait()
        data_copy(q).wait()
        total = None
        for h in range(4):
            term = lax.dot_general(slopes[h % 2, 2 * q + h // 2],
                                   dbuf[pl.ds(pl.multiple_of(q * m, m), m), h * half : (h + 1) * half], NT,
                                   preferred_element_type=F32)
            total = term if total is None else total + term
        a_ref[...] += total

        def noise_rows(i, _):
            at = pl.ds(pl.multiple_of(i * 32, 32), 32)
            value = squares(slopes[0, 2 * q, at, :])
            for h in range(1, 4):
                value = value + squares(slopes[h % 2, 2 * q + h // 2, at, :])
            nsq[at, :] += value
            return 0

        def data_rows(i, _):
            at = pl.ds(pl.multiple_of(i * 32, 32), 32)
            dsq[at, :] += squares(dbuf[pl.ds(pl.multiple_of(q * m + i * 32, 32), 32), :])
            return 0

        lax.fori_loop(0, n // 32, noise_rows, 0)
        lax.fori_loop(0, m // 32, data_rows, 0)
        return 0

    lax.fori_loop(0, 4, cost_step, 0)
    noise_sq = jnp.sum(nsq[...], axis=1, keepdims=True)
    data_sq = jnp.sum(dsq[...].T, axis=0, keepdims=True)
    a_ref[...] = (noise_sq + data_sq - 2.0 * a_ref[...]) * (1.0 / (width * EPSILON))
    base = -math.log(tokens)
    at("c4")

    def rows_swap(it):
        for d in range(1, n_rows):
            rcopy(csend.at[it], crecv.at[it, d - 1], cs.at[it], cr.at[it], (lax.rem(row + d, n_rows), col))

    def cols_swap(it):
        for d in range(1, n_cols):
            rcopy(rsend.at[it], rrecv.at[it, d - 1], rs.at[it], rr.at[it], (row, lax.rem(col + d, n_cols)))

    def await_all(ref, sem):
        pltpu.make_async_copy(ref, ref, sem).wait()

    def merge(got, top, tot):
        gt = got[:, 0, :]
        best = jnp.maximum(top, jnp.max(gt, axis=0, keepdims=True))
        total = tot * jnp.exp(top - best) + jnp.sum(got[:, 1, :] * jnp.exp(gt - best), axis=0, keepdims=True)
        return base - (best + jnp.log(total))

    def when(condition, *points):
        @pl.when(condition)
        def _():
            for point in points:
                at(point)

    def sweep(it, fg):
        x = fg[0] - a_ref[...]
        top = jnp.max(x, axis=0, keepdims=True)
        tot = jnp.sum(jnp.exp(x - top), axis=0, keepdims=True)
        csend[it, 0:1, :] = top
        csend[it, 1:2, :] = tot
        rows_swap(it)
        for i in range(ITERS):
            when(it == i, ("k0c", "k1c", "k2c")[i])
        await_all(crecv.at[it], cr.at[it])
        g = merge(crecv[it], top, tot)

        x = g - a_ref[...]
        top = jnp.max(x, axis=1, keepdims=True)
        tot = jnp.sum(jnp.exp(x - top), axis=1, keepdims=True)
        top, tot = flat(top, tot)
        rsend[it, 0:1, :] = top
        rsend[it, 1:2, :] = tot
        cols_swap(it)
        for i in range(ITERS):
            when(it == i, ("k0r", "k1r", "k2r")[i])
        await_all(rrecv.at[it], rr.at[it])
        return tall(merge(rrecv[it], top, tot), n), g

    f, g = lax.fori_loop(0, ITERS, sweep, (jnp.zeros((n, 1), F32), jnp.zeros((1, m), F32)))
    p_ref[...] = (float(tokens) * jnp.exp(f + g - a_ref[...])).astype(BF16)
    for it in range(ITERS):
        await_all(crecv.at[it], cs.at[it])
        await_all(rrecv.at[it], rs.at[it])

    def at_x(d, k):
        return (row, ring(xx + d) * 2 + k)

    def reduce_copy(t, u, i):
        lo, hi = pl.ds(0, hn), pl.ds(hn, hn)
        if not isinstance(i, int):
            src, dst, to = sibs.at[u, i], sibr.at[u, i], at_x(0, 1 - core)
        else:
            src, dst, d = {
                4: (outs.at[u, 0, lo], rh.at[u, 0], 1),
                5: (outs.at[u, 0, hi], rh.at[u, 1], -1),
                6: (outs.at[u, 1, hi], rf.at[u, 0, hi], 1),
                7: (outs.at[u, 2, lo], rf.at[u, 1, lo], -1),
                8: (outs.at[u, 1, lo], rf.at[u, 0, lo], 1),
                9: (outs.at[u, 2, hi], rf.at[u, 1, hi], -1),
            }[i]
            to = at_x(d, core)
        return rdesc(src, dst, xs.at[t, u, i], xr.at[t, u, i], to)

    def cols_reduce(make, t, u):
        def offset(i):
            return jnp.where(i == 0, 2, jnp.where(i == 3, 0, 2 * i - 1))

        def twin_step(i, _):
            sibs[u, i] = make(ring(xx + offset(i)) * 2 + 1 - core, u).astype(BF16)
            reduce_copy(t, u, i).start()
            return 0

        def block_step(i, _):
            d = offset(i)
            value = make(ring(xx + d) * 2 + core, u)
            reduce_copy(t, u, i).wait_recv()
            value = value + sibr[u, i].astype(F32)
            own[u] = value
            outs[u, i] = value.astype(BF16)

            @pl.when(i == 0)
            def _():
                reduce_copy(t, u, 4).start()
                reduce_copy(t, u, 5).start()

            @pl.when(i == 1)
            def _():
                reduce_copy(t, u, 6).start()

            @pl.when(i == 2)
            def _():
                reduce_copy(t, u, 7).start()

            return 0

        def twins():
            lax.fori_loop(0, 4, twin_step, 0)

        def blocks():
            lax.fori_loop(0, 4, block_step, 0)

        return twins, blocks

    def reduce_middle(t, u):
        reduce_copy(t, u, 4).wait_recv()
        outs[u, 1, 0:hn] = (outs[u, 1, 0:hn].astype(F32) + rh[u, 0].astype(F32)).astype(BF16)
        reduce_copy(t, u, 8).start()
        reduce_copy(t, u, 5).wait_recv()
        outs[u, 2, hn:n] = (outs[u, 2, hn:n].astype(F32) + rh[u, 1].astype(F32)).astype(BF16)
        reduce_copy(t, u, 9).start()

    def reduced(t, u):
        for i in (6, 7, 8, 9):
            reduce_copy(t, u, i).wait_recv()
        value = own[u] + rf[u, 0].astype(F32) + rf[u, 1].astype(F32)
        for i in range(4):
            reduce_copy(t, u, jnp.int32(i)).wait_send()
        for i in range(4, 10):
            reduce_copy(t, u, i).wait_send()
        return value

    def slot(d, k):
        return ring(xx + d) * 2 + k

    other = 1 - core

    def visit(j):
        d = jnp.where(j < 2, 0, jnp.where(j >= 6, 2, 2 * lax.rem(j, 2) - 1))
        k = jnp.where((j == 1) | (j == 4) | (j == 5) | (j == 7), other, core)
        return slot(d, k)

    def spread(ref, t, u):
        def copy(i):
            lo, hi = pl.ds(0, hn), pl.ds(hn, hn)
            twin = at_x(0, other)
            src, to = {
                0: (ref.at[u, col], at_x(1, core)),
                1: (ref.at[u, col], at_x(-1, core)),
                2: (ref.at[u, col], twin),
                3: (ref.at[u, slot(-1, core), lo], at_x(1, core)),
                4: (ref.at[u, slot(1, core), hi], at_x(-1, core)),
                5: (ref.at[u, slot(-1, core)], twin),
                6: (ref.at[u, slot(1, core)], twin),
                7: (ref.at[u, slot(2, core), lo], twin),
                8: (ref.at[u, slot(2, core), hi], twin),
            }[i]
            return rdesc(src, src, ug_s.at[t, u, i], ug_r.at[t, u, i], to)

        def begin():
            for i in range(3):
                copy(i).start()

        def middle():
            copy(0).wait_recv()
            copy(3).start()
            copy(5).start()
            copy(1).wait_recv()
            copy(4).start()
            copy(6).start()

        def finish():
            copy(3).wait_recv()
            copy(7).start()
            copy(4).wait_recv()
            copy(8).start()

        def got(*which):
            for i in which:
                copy(i).wait_recv()

        def close():
            for i in range(9):
                copy(i).wait_send()

        return begin, middle, finish, got, close

    tiles = ffd // 256

    def tile(j):
        return pl.ds(pl.multiple_of(j * 256, 256), 256)

    def rows_of(i, u, size):
        return pl.ds(pl.multiple_of(i * share + u * size, size), size)

    def target_block(fb, u):
        rows_at = pl.ds(pl.multiple_of(fb // 2 * m, m), m)
        lanes = pl.ds(pl.multiple_of(lax.rem(fb, 2) * share + u * half, half), half)
        return jnp.dot(p_ref[...], dbuf[rows_at, lanes], preferred_element_type=F32)

    t = tall(times_ref[...][None, :], n)

    def make_state(value, u):
        target = value.astype(BF16)
        target_ref[:, u * half : (u + 1) * half] = target
        target = target.astype(F32)
        noise = slopes[u, col].astype(F32)
        lanes = pl.ds(pl.multiple_of(col * share + u * half, half), half)
        st = (1.0 - t) * noise + t * target + t * embed_ref[:, lanes]
        latents[u, col] = (st * gain_ref[:, lanes]).astype(BF16)
        state[:, u * half : (u + 1) * half] = st - (target - noise)
        return jnp.sum(st * st, axis=1, keepdims=True)

    hb0, hm0, hf0, hg0, hc0 = spread(latents, 0, 0)
    hb1, hm1, hf1, hg1, hc1 = spread(latents, 0, 1)

    at("t0")
    twins0, blocks0 = cols_reduce(target_block, 0, 0)
    twins1, blocks1 = cols_reduce(target_block, 0, 1)
    twins0()
    blocks0()
    twins1()
    reduce_middle(0, 0)
    at("t2")
    blocks1()
    reduce_middle(0, 1)
    at("t4")
    part = make_state(reduced(0, 0), 0)
    hb0()
    at("t5")
    part = part + make_state(reduced(0, 1), 1)
    part, _ = flat(part, part)
    rsend[ITERS, 0:1, :] = part
    rsend[ITERS, 1:2, :] = part
    cols_swap(ITERS)
    hm0()
    hb1()
    at("h0")
    hid[...] = jnp.zeros_like(hid)

    def hidden_step(j, _):
        @pl.when(j == 1)
        def _():
            at("h1")
            hf0()
            hm1()
            at("h2")
            hg0(2)
            hg1(2)

        @pl.when(j == 3)
        def _():
            hf1()

        @pl.when(j == 4)
        def _():
            at("h3")
            hg0(5)
            hg1(5)

        @pl.when(j == 5)
        def _():
            hg0(6)
            hg1(6)

        @pl.when(j == 7)
        def _():
            at("h4")
            hg0(7, 8)
            hg1(7, 8)

        i = visit(j)
        hid[...] += (jnp.dot(latents[0, i], win[rows_of(i, 0, half), :], preferred_element_type=F32)
                     + jnp.dot(latents[1, i], win[rows_of(i, 1, half), :], preferred_element_type=F32))
        return 0

    lax.fori_loop(0, n_cols, hidden_step, 0)
    hc0()
    hc1()
    await_all(rrecv.at[ITERS], rr.at[ITERS])
    await_all(rrecv.at[ITERS], rs.at[ITERS])
    square = part + jnp.sum(rrecv[ITERS][:, 0, :], axis=0, keepdims=True)
    scale = tall(lax.rsqrt(square / width + 1e-6), n)

    def gelu_step(j, _):
        h = hid[:, tile(j)] * scale
        c = math.sqrt(2.0 / math.pi)
        h2 = h * h
        th = jnp.tanh(c * (h + 0.044715 * (h2 * h)))
        act[:, tile(j)] = (0.5 * h * (1.0 + th)).astype(BF16)
        slope_of = 0.5 * (1.0 + th) + 0.5 * h * (1.0 - th * th) * (c * (1.0 + (3 * 0.044715) * h2))
        hid[:, tile(j)] = slope_of * scale
        return 0

    lax.fori_loop(0, tiles, gelu_step, 0)
    at("v0")

    def pair(ref, i, u, at):
        lo = ref[pl.ds(pl.multiple_of(i * share + u * eighth, eighth), eighth), at]
        hi = ref[pl.ds(pl.multiple_of(i * share + half + u * eighth, eighth), eighth), at]
        return jnp.concatenate([lo, hi], axis=0)

    def velocity_block(fb, u):
        return lax.dot_general(act[...], pair(wout, fb, u, slice(None)), NT, preferred_element_type=F32)

    def make_slope(value, u):
        lo = state[:, u * eighth : (u + 1) * eighth]
        hi = state[:, half + u * eighth : half + (u + 1) * eighth]
        slopes[u, col] = ((jnp.concatenate([lo, hi], axis=1) + value) * (1.0 / math.sqrt(tokens))).astype(BF16)

    TN = (((0,), (0,)), ((), ()))

    def use_slope(i, u):
        value = lax.dot_general(slopes[u, i], act[...], TN, preferred_element_type=F32).astype(BF16)
        dbuf[pl.ds(pl.multiple_of(i * share + u * eighth, eighth), eighth), :] = value[:eighth]
        dbuf[pl.ds(pl.multiple_of(i * share + half + u * eighth, eighth), eighth), :] = value[eighth:]

    def rx_at(ref, base, unit, path, j, part=None):
        high = unit[1]
        off = high // 2 if part == 1 else 0
        size = high if part is None else high // 2
        return ref.at[pl.ds(base + (path * 16 + j) * high + off, size)]

    def shift(w, path, i):
        ref = (dbuf, dbuf, win)[w]
        unit = (low, up, wide)[w]
        f, s = here(path)
        if i < 4:
            e, axis, d = (2, 1, 3, 0)[i], "f", 1 if i < 2 else -1
            src, dst = (f + 2, s + e, None), (i, None)
        elif i < 12:
            e, axis, d = i % 4, "f", 1 if i < 8 else -1
            src, dst = (f + d, s + e, None), (i, None)
        else:
            axis, d = "s", 1 if i % 2 == 0 else -1
            src, dst = {
                12: ((f, s + 2, 0), (12, 0)), 13: ((f, s + 2, 1), (12, 1)),
                14: ((f, s + 1, 1), (13, 1)), 15: ((f, s - 1, 0), (14, 0)),
                16: ((f, s + 1, 0), (13, 0)), 17: ((f, s - 1, 1), (14, 1)),
            }[i]
        return rdesc(piece(ref, unit, path, *src), landing(w, path, *dst),
                     gr_s.at[w, path, i], gr_r.at[w, path, i], toward(path, axis, d))

    def landing(w, path, j, part=None):
        return rx_at((rx, rx, wout)[w], (0, width // 2, 0)[w], (low, up, wide)[w], path, j, part)

    def add(at, *more):
        def rows_step(r, _):
            rows = pl.ds(pl.multiple_of(r * 32, 32), 32)
            value = at[rows, :].astype(F32)
            for one in more:
                value = value + one[rows, :].astype(F32)
            at[rows, :] = value.astype(BF16)
            return 0

        lax.fori_loop(0, at.shape[0] // 32, rows_step, 0)

    def scatter(w, step):
        ref = (dbuf, dbuf, win)[w]
        unit = (low, up, wide)[w]
        high = unit[1]
        if step == 1:
            for i in (0, 1, 2, 3, 4, 7, 9, 10):
                for path in range(2):
                    shift(w, path, i).start()
        both = [(path, *here(path)) for path in range(2)]
        if step == 2:
            for j in range(2):
                for path, f, s in both:
                    for d, i, e in ((1, j, (2, 1)[j]), (-1, 2 + j, (3, 0)[j])):
                        shift(w, path, i).wait_recv()
                        add(piece(ref, unit, path, f + d, s + e), landing(w, path, i))
                        shift(w, path, (4 if d == 1 else 8) + e).start()
        if step == 3:
            for e in ORDER:
                for path, f, s in both:
                    shift(w, path, 4 + e).wait_recv()
                    shift(w, path, 8 + e).wait_recv()
                    add(piece(ref, unit, path, f, s + e), landing(w, path, 4 + e), landing(w, path, 8 + e))
                    for i in {2: (12, 13), 1: (14,), 3: (15,), 0: ()}[e]:
                        shift(w, path, i).start()
        for path, f, s in both:
            if step == 4:
                shift(w, path, 12).wait_recv()
                add(piece(ref, unit, path, f, s + 1, 0), landing(w, path, 12, 0))
                shift(w, path, 16).start()
                shift(w, path, 13).wait_recv()
                add(piece(ref, unit, path, f, s - 1, 1), landing(w, path, 12, 1))
                shift(w, path, 17).start()
            if step == 5:
                for i in range(14, 18):
                    shift(w, path, i).wait_recv()
                value = (piece(ref, unit, path, f, s)[...].astype(F32) + landing(w, path, 13)[...].astype(F32)
                         + landing(w, path, 14)[...].astype(F32))
                if w < 2:
                    final[w, path * high : (path + 1) * high, :] = value
                    if path == 1:
                        gout_ref[:, w * 2 * high : (w + 1) * 2 * high] = final[w].T.astype(BF16)
                else:
                    gin_ref[path * high : (path + 1) * high, :] = value.astype(BF16)
                for i in range(18):
                    shift(w, path, i).wait_send()

    sb0, sm0, sf0, sg0, sc0 = spread(slopes, 1, 0)
    sb1, sm1, sf1, sg1, sc1 = spread(slopes, 1, 1)

    def velocity_half(u, _):
        when(u == 1, "v1")
        twins, blocks = cols_reduce(velocity_block, 1, u)
        twins()
        blocks()
        reduce_middle(1, u)
        return 0

    lax.fori_loop(0, 2, velocity_half, 0)
    make_slope(reduced(1, 0), 0)
    sb0()

    def slope_step(jj, _):
        def on(number, *calls):
            @pl.when(jj == number)
            def _():
                for call in calls:
                    call()

        on(1, lambda: make_slope(reduced(1, 1), 1), sm0, sb1, lambda: sg0(2))
        on(4, sf0, lambda: sg0(5))
        on(5, lambda: sg0(6))
        on(7, lambda: sg0(7, 8))
        on(8, lambda: scatter(0, 1), sm1)
        on(9, lambda: sg1(2))
        on(12, sf1, lambda: sg1(5))
        on(13, lambda: sg1(6))
        on(15, lambda: sg1(7, 8))
        use_slope(visit(lax.rem(jj, 8)), jj // 8)
        return 0

    lax.fori_loop(0, 16, slope_step, 0)
    scatter(1, 1)
    sc0()
    sc1()
    scatter(0, 2)

    every = slice(None)
    back[...] = jnp.zeros_like(back)

    def back_step(i, _):
        back[...] += (jnp.dot(slopes[0, i], pair(wout, i, 0, every), preferred_element_type=F32)
                      + jnp.dot(slopes[1, i], pair(wout, i, 1, every), preferred_element_type=F32))
        return 0

    lax.fori_loop(0, n_cols, back_step, 0)
    for w in range(3):
        for path in range(2):
            for i in range(20):
                carry(w, path, i).wait_send()
    for path in range(2):
        for d in (1, -1):
            pl.semaphore_signal(credit, inc=1, device_id=toward(path, "f", d), device_id_type=MESH)
    scatter(1, 2)
    sh[...] = (back[...] * hid[...]).astype(BF16)

    def in_step(i, _):
        win[pl.ds(pl.multiple_of(i * half, half), half), :] = lax.dot_general(
            latents[lax.rem(i, 2), i // 2], sh[...], TN, preferred_element_type=F32).astype(BF16)
        return 0

    lax.fori_loop(0, 2 * n_cols, in_step, 0)
    pl.semaphore_wait(credit, 4)
    scatter(2, 1)
    scatter(0, 3)
    scatter(2, 2)
    scatter(1, 3)
    scatter(0, 4)
    scatter(2, 3)
    scatter(1, 4)
    scatter(2, 4)
    scatter(0, 5)
    scatter(1, 5)
    scatter(2, 5)


def hand_out(a, b, c, x, y, z, *rest):
    sem = rest[3]
    ins = [pltpu.make_async_copy(s, v, sem.at[i]) for i, (s, v) in enumerate(zip((a, b, c), rest))]
    outs = [pltpu.make_async_copy(v, d, sem.at[3 + i]) for i, (v, d) in enumerate(zip(rest, (x, y, z)))]
    for c in ins:
        c.start()
    for i in range(3):
        ins[i].wait()
        outs[i].start()
    for c in outs:
        c.wait()


def per_device(noise, data, times, time_embed, norm_gain, w_in, w_out):
    n, width = noise.shape
    m = data.shape[0]
    wr, ffd = w_in.shape
    share = width // 8
    half = share // 2
    vm = pl.BlockSpec(memory_space=pltpu.VMEM)
    hbm = pl.BlockSpec(memory_space=pl.ANY)
    dma = pltpu.SemaphoreType.DMA
    outs = pl.pallas_call(
        kernel,
        out_shape=(
            jax.ShapeDtypeStruct((n, share), BF16),
            jax.ShapeDtypeStruct((wr, ffd), BF16),
            jax.ShapeDtypeStruct((ffd, wr), BF16),
        ),
        in_specs=[hbm, hbm, vm, vm, vm, hbm, vm],
        out_specs=(vm, vm, vm),
        scratch_shapes=[
            pltpu.VMEM((2, 8, n, half), BF16),
            pltpu.VMEM((width, ffd), BF16),
            pltpu.VMEM((width, ffd), BF16),
            pltpu.VMEM((width, ffd), BF16),
            pltpu.VMEM((width, ffd), BF16),
            pltpu.VMEM((2, 8, n, half), BF16),
            pltpu.VMEM((n, ffd), BF16),
            pltpu.VMEM((n, ffd), F32),
            pltpu.VMEM((n, ffd), F32),
            pltpu.VMEM((n, m), F32),
            pltpu.VMEM((n, m), BF16),
            pltpu.VMEM((n, share), F32),
            pltpu.VMEM((n, ffd), BF16),
            pltpu.VMEM((2, 4, n, half), BF16),
            pltpu.VMEM((2, 4, n, half), BF16),
            pltpu.VMEM((2, 4, n, half), BF16),
            pltpu.VMEM((2, 2, n // 2, half), BF16),
            pltpu.VMEM((2, 2, n, half), BF16),
            pltpu.VMEM((2, n, half), F32),
            pltpu.VMEM((n, 128), F32),
            pltpu.VMEM((m, 128), F32),
            pltpu.VMEM((2, wr // 2, ffd), F32),
            pltpu.VMEM((ITERS, 2, m), F32),
            pltpu.VMEM((ITERS, 15, 2, m), F32),
            pltpu.VMEM((ITERS + 1, 2, n), F32),
            pltpu.VMEM((ITERS + 1, 7, 2, n), F32),
            dma((ITERS,)), dma((ITERS,)), dma((ITERS + 1,)), dma((ITERS + 1,)),
            dma((3, 2, 20)), dma((3, 2, 20)),
            dma((2, 2, 10)), dma((2, 2, 10)),
            dma((2, 2, 9)), dma((2, 2, 9)),
            dma((3, 2, 18)), dma((3, 2, 18)),
            dma((21,)),
            pltpu.SemaphoreType.REGULAR,
        ],
        compiler_params=pltpu.CompilerParams(
            collective_id=0, has_side_effects=True, vmem_limit_bytes=62 * 2**20
        ),
    )(noise, data, times, time_embed[None, :], norm_gain[None, :], w_in, w_out)
    return pl.pallas_call(
        hand_out,
        out_shape=tuple(jax.ShapeDtypeStruct(o.shape, o.dtype) for o in outs),
        in_specs=[hbm] * 3,
        out_specs=(hbm,) * 3,
        scratch_shapes=[pltpu.VMEM(o.shape, o.dtype) for o in outs] + [dma((6,))],
    )(*outs)


def solution(mesh):
    in_specs = (
        P("rows", None),
        P("cols", None),
        P("rows"),
        P(),
        P(),
        P("rows", "cols"),
        P("cols", "rows"),
    )
    out_specs = (P("rows", "cols"), P("rows", "cols"), P("cols", "rows"))
    return jax.shard_map(
        per_device, mesh=mesh, in_specs=in_specs, out_specs=out_specs, check_vma=False
    )
```
